256 devices in a mesh: pipe: 8 (over z_lo, core), dp: 8 (over x, z_hi), mp: 4 (over y).
Axes of the slice: x: 4, y: 4, z: 8 (z_hi: 2, z_lo: 4; z = z_hi * 4 + z_lo), core: 2. Of those that a mesh axis runs over, the one named last changes fastest.
Arguments:
- acts: bfloat16 [16, 64, 6144], P('dp', None, 'mp'), may hold values from -6 to 6
- out_grad: bfloat16 [16, 64, 6144], P('dp', None, 'mp'), may hold values from -6 to 6
- value_weight: bfloat16 [8, 6144, 6144], P('pipe', 'dp', 'mp'), may hold values from -2 to 2
- output_weight: bfloat16 [8, 6144, 6144], P('pipe', 'mp', 'dp'), may hold values from -0.078125 to 0.078125
- decay: float32 [8, 48], P('pipe', 'mp'), may hold values from 0.6 to 0.99
Outputs:
- segment_out: bfloat16 [8, 16, 64, 6144], P('pipe', 'dp', None, 'mp')
- segment_in_grad: bfloat16 [8, 16, 64, 6144], P('pipe', 'dp', None, 'mp')
- value_grad: bfloat16 [8, 6144, 6144], P('pipe', 'dp', 'mp')
- output_grad: bfloat16 [8, 6144, 6144], P('pipe', 'mp', 'dp')
The draws below stay inside these ranges and needn't reach their ends.
All inputs are finite; a program needn't handle non-finite values.
Results may differ from the reference program's by a relative error of at most 0.03.
Values may be sent and summed in bfloat16 or wider, within the bound.
A program may use at most 192 MiB of HBM per device.

```python
import jax
import jax.numpy as jnp
from jax import lax

D = 6144
HEADS = 48
HD = 128
MBT = 64
HV = 6144
BATCHES = 16
N_PIPE = 8


def weight_rows(key, rise, common_key, noise_key):
    places = jnp.arange(D).astype(jnp.float32) / D
    row_scale = jnp.exp(places * jnp.log(rise))
    norm_scale = jnp.sqrt(jnp.mean(row_scale * row_scale))
    common = jnp.clip(jax.random.normal(common_key, (N_PIPE, 1, HV), jnp.float32), -3.0, 3.0)
    noise = jnp.clip(jax.random.normal(noise_key, (N_PIPE, D, HV), jnp.float32), -3.0, 3.0)
    entries = (common + noise) * (row_scale / norm_scale)[None, :, None] / jnp.sqrt(jnp.float32(D))
    return jnp.clip(entries, -2.0, 2.0)


def draw_value_weight(key, part):
    key = jax.random.fold_in(key, 7)
    common_key = jax.random.fold_in(key, 1)
    noise_key = jax.random.fold_in(key, 2)
    return weight_rows(key, 4.0, common_key, noise_key).astype(jnp.bfloat16)


def block_levels(key, extent, shards, least, largest):
    def one(dim, blocks):
        steps = jax.random.uniform(jax.random.fold_in(jax.random.fold_in(key, 6), dim), (blocks,), jnp.float32, least / len(shards), largest / len(shards))
        return jnp.repeat(jnp.exp(steps), extent[dim] // blocks).reshape((-1,) + (1,) * (len(extent) - dim - 1))

    gain = one(*shards[0])
    for cut in shards[1:]:
        gain = gain * one(*cut)
    return gain


def normal_values(key, dims, width, reach, shards=(), held_as=jnp.bfloat16):
    factor_of = block_levels(key, dims, shards, -0.22, 0.18) if shards else 1.0
    array = jax.random.normal(key, dims, jnp.float32) * width * factor_of
    return jnp.minimum(jnp.maximum(array, -reach), reach).astype(held_as)


def setup_inputs(seed: int = 0) -> dict:
    key_list = jax.random.split(jax.random.key(seed), 6)
    return {
        "acts": normal_values(key_list[0], (BATCHES, MBT, D), 1.0, 6.0, ((0, 8), (2, 4))),
        "out_grad": normal_values(key_list[1], (BATCHES, MBT, D), 1.0, 6.0, ((0, 8), (2, 4))),
        "value_weight": draw_value_weight(jax.random.fold_in(key_list[5], 71), 0),
        "output_weight": normal_values(key_list[3], (N_PIPE, HV, D), HV ** -0.5, 0.078125, ((0, 8), (1, 4), (2, 8))),
        "decay": jnp.clip(0.6 + 0.39 * jax.random.uniform(key_list[4], (N_PIPE, HEADS), jnp.float32) ** block_levels(key_list[4], (N_PIPE, HEADS), ((0, 8), (1, 4)), -0.2, 0.2), 0.6, 0.99),
    }


EPSILON = 1e-05

def mixing_table(rates, length):
    places = jnp.arange(length).astype(jnp.float32)
    offset = places[:, None] - places[None, :]
    lower = offset >= 0.0
    powers = jnp.exp(jnp.maximum(offset, 0.0)[None, :, :] * jnp.log(rates)[:, None, None])
    scales = jnp.sqrt(1.0 - rates * rates)[:, None, None]
    return jnp.where(lower[None, :, :], powers * scales, 0.0)

def reference(acts, out_grad, value_weight, output_weight, decay):
    batches = acts.shape[0]
    length = acts.shape[1]
    hidden = acts
    saved = []
    outputs = []
    for section in range(N_PIPE):
        table = mixing_table(decay[section], length)
        floats = hidden.astype(jnp.float32).reshape(-1, D)
        centered = floats - lax.optimization_barrier(jnp.mean(floats, axis=1, keepdims=True))
        inverse = lax.rsqrt(lax.optimization_barrier(jnp.mean(centered * centered, axis=1, keepdims=True)) + EPSILON)
        scaled = centered * inverse
        normed = scaled.astype(jnp.bfloat16)
        values = jnp.dot(normed, value_weight[section], preferred_element_type=jnp.float32).astype(jnp.bfloat16)
        heads_in = values.astype(jnp.float32).reshape(batches, length, HEADS, HD)
        mixed = jnp.einsum('hts,bshd->bthd', table, heads_in).reshape(-1, HV).astype(jnp.bfloat16)
        branch = jnp.dot(mixed, output_weight[section], preferred_element_type=jnp.float32)
        hidden = (floats + branch).astype(jnp.bfloat16).reshape(batches, length, D)
        saved.append((scaled, inverse, normed, mixed, table))
        outputs.append(hidden)
    grad_now = out_grad
    in_grads = [None] * N_PIPE
    value_grads = [None] * N_PIPE
    output_grads = [None] * N_PIPE
    for section in range(N_PIPE - 1, -1, -1):
        scaled, inverse, normed, mixed, table = saved[section]
        flat_grad = grad_now.reshape(-1, D)
        mixed_grad = jnp.dot(flat_grad, output_weight[section].T, preferred_element_type=jnp.float32).astype(jnp.bfloat16)
        back_heads = mixed_grad.astype(jnp.float32).reshape(batches, length, HEADS, HD)
        values_grad = jnp.einsum('hts,bthd->bshd', table, back_heads).reshape(-1, HV).astype(jnp.bfloat16)
        normed_grad = jnp.dot(values_grad, value_weight[section].T, preferred_element_type=jnp.float32)
        first_mean = lax.optimization_barrier(jnp.mean(normed_grad, axis=1, keepdims=True))
        second_mean = lax.optimization_barrier(jnp.mean(normed_grad * scaled, axis=1, keepdims=True))
        hidden_grad = inverse * (normed_grad - first_mean - scaled * second_mean)
        new_grad = (flat_grad.astype(jnp.float32) + hidden_grad).astype(jnp.bfloat16)
        value_grads[section] = jnp.dot(normed.T, values_grad, preferred_element_type=jnp.float32).astype(jnp.bfloat16)
        output_grads[section] = jnp.dot(mixed.T, flat_grad, preferred_element_type=jnp.float32).astype(jnp.bfloat16)
        grad_now = new_grad.reshape(batches, length, D)
        in_grads[section] = grad_now
    return (jnp.stack(outputs), jnp.stack(in_grads), jnp.stack(value_grads), jnp.stack(output_grads))
```

```python
import functools

import jax
import jax.numpy as jnp
from jax import lax
from jax.experimental import pallas as pl
from jax.experimental.pallas import tpu as pltpu
from jax.sharding import PartitionSpec as P

EPSILON = 1e-05
F32 = jnp.float32
BF16 = jnp.bfloat16
MESH = pl.DeviceIdType.MESH

TOKENS = 1024
MBT = 64
ROWS = 64
CHUNKS = TOKENS // ROWS
OWN = ROWS // 4
WIDTH = 6144
BLK = 768
VAL = 1536
PIECE = 384
SECTIONS = 8
LANES = 128

FORWARD_ORDER = ((1, 0), (3, 1), (5, 2), (2, 0), (4, 1))
BACKWARD_ORDER = ((1, 0), (3, 1), (5, 2), (2, 0), (4, 1))


def send(src, dst, send_sem, recv_sem, **device):
    pltpu.make_async_remote_copy(
        src_ref=src,
        dst_ref=dst,
        send_sem=send_sem,
        recv_sem=recv_sem,
        device_id=device,
        device_id_type=MESH,
    ).start()


def await_bytes(ref, sem):
    pltpu.make_async_copy(ref, ref, sem).wait()


def send_or_copy(here, src, dst, send_sem, recv_sem, **device):
    @pl.when(here)
    def _():
        pltpu.make_async_copy(src, dst, recv_sem).start()

    @pl.when(jnp.logical_not(here))
    def _():
        send(src, dst, send_sem, recv_sem, **device)


def run_phases(order, phases):
    last = max(lag for _, lag in order)

    def window(step, carry):
        for which, lag in order:
            chunk = step - lag
            pl.when((chunk >= 0) & (chunk < CHUNKS))(functools.partial(phases[which], chunk))
        return carry

    lax.fori_loop(0, CHUNKS + last, window, 0)


def to_rows(first, second):
    lane = lax.broadcasted_iota(jnp.int32, (ROWS, LANES), 1)
    tile = jnp.where(lane == 0, first, jnp.where(lane == 1, second, 0.0))
    if ROWS < LANES:
        tile = jnp.concatenate([tile, jnp.zeros((LANES - ROWS, LANES), F32)], axis=0)
    return tile.T[:8]


def kernel(
    acts,
    out_grad,
    wv,
    wo,
    decay,
    seg_out,
    seg_grad,
    value_grad,
    output_grad,
    hid,
    part,
    part_in,
    swap,
    swap_in,
    mixed,
    branch,
    branch_in,
    hid_out,
    out_land,
    grad,
    gpart,
    gpart_in,
    gswap,
    gswap_in,
    vgrad,
    gbranch,
    gbranch_in,
    grad_out,
    grad_land,
    stats,
    sums,
    sums_in,
    vals,
    norm,
    abx,
    aby,
    aby_in,
    table,
    tile,
    normed_t,
    mixed_t,
    recv,
    sent,
    once,
):
    p = lax.axis_index("pipe")
    d = lax.axis_index("dp")
    m = lax.axis_index("mp")
    x = d // 2
    z = d % 2
    (H_IN, ST_IN, P_IN, S_IN, M_IN, Y_IN, G_IN, GP_IN, GS_IN, V_IN, GY_IN, AX_IN, AY_IN) = range(13)
    (ST, PO, SW, MX, YO, HO, OO, GPO, GSW, VX, GYO, GO, GOO, AX, AY) = range(15)
    SUMS_R, OUT_R, GOUT_R, SUMS_S, FIRST_S = range(5)

    def cols_of(which):
        return pl.ds(pl.multiple_of(which * PIECE, LANES), PIECE)

    mine = pl.ds(pl.multiple_of(m * OWN, OWN), OWN)

    barrier = pltpu.get_barrier_semaphore()

    def greet(k, carry):
        dd = (d + k // 4) % 8
        mm = (m + k % 4) % 4
        pl.semaphore_signal(barrier, inc=1, device_id={"dp": dd, "mp": mm}, device_id_type=MESH)
        return carry

    lax.fori_loop(1, 32, greet, 0)

    @pl.when(p < SECTIONS - 1)
    def _():
        for k in range(4):
            pl.semaphore_signal(
                barrier, inc=1, device_id={"pipe": p + 1, "mp": (m + k) % 4}, device_id_type=MESH
            )

    @pl.when(p > 0)
    def _():
        for k in range(4):
            pl.semaphore_signal(
                barrier, inc=1, device_id={"pipe": p - 1, "mp": (m + k) % 4}, device_id_type=MESH
            )

    col_sum = jnp.sum(wv[0].astype(F32), axis=0, keepdims=True)
    sums[...] = jnp.broadcast_to(col_sum, (8, VAL))
    tile[...] = jnp.zeros((LANES, LANES), F32)
    row_id = lax.broadcasted_iota(jnp.int32, (MBT, MBT), 0).astype(F32)
    col_id = lax.broadcasted_iota(jnp.int32, (MBT, MBT), 1).astype(F32)
    for k in range(3):
        rate = jnp.full((MBT, MBT), decay[0, 3 * x + k], F32)
        scale = jnp.sqrt(1.0 - rate * rate)
        log_rate = jnp.log(rate)
        for way in range(2):
            offset = row_id - col_id if way == 0 else col_id - row_id
            power = jnp.exp(jnp.maximum(offset, 0.0) * log_rate) * scale
            table[way, k] = jnp.where(offset >= 0.0, power, 0.0).astype(BF16)

    inner = (p > 0) & (p < SECTIONS - 1)

    @pl.when(inner)
    def _():
        pl.semaphore_wait(barrier, 39)

    @pl.when(jnp.logical_not(inner))
    def _():
        pl.semaphore_wait(barrier, 35)

    def first_inputs(source, landing, sem):
        for b in range(2):
            start = (2 * d + b) * MBT
            chunk = start // ROWS
            row = pl.multiple_of(start % ROWS, MBT)
            for zz in range(2):
                for k in range(4):
                    dd = 2 * m + zz
                    mm = (m + k) % 4
                    send_or_copy(
                        (dd == d) & (mm == m),
                        source.at[b, :, pl.ds(zz * BLK, BLK)],
                        landing.at[chunk, pl.ds(row, MBT)],
                        once.at[FIRST_S],
                        recv.at[sem, chunk],
                        dp=dd,
                        mp=mm,
                    )

    @pl.when(p == 0)
    def _():
        first_inputs(acts, hid, H_IN)

    for k in range(1, 8):
        dd = (d + k) % 8
        send(
            sums.at[:, cols_of(dd // 2)],
            sums_in.at[k],
            once.at[SUMS_S],
            once.at[SUMS_R],
            dp=dd,
        )
    sums_in[0] = sums[:, cols_of(x)]

    @pl.when(p == SECTIONS - 1)
    def _():
        first_inputs(out_grad, grad, G_IN)

    await_bytes(sums_in.at[pl.ds(1, 7)], once.at[SUMS_R])

    def spread_pieces(c, source, landing, put, sem):
        for k in (2, 1, 3):
            send(
                source.at[c, k],
                landing.at[c, k - 1],
                sent.at[put, c],
                recv.at[sem, c],
                dp=2 * ((x + k) % 4) + z,
            )

    def gather_pieces(c, source, put, sem):
        for k in (2, 1, 3):
            send(
                source.at[c, x],
                source.at[c, x],
                sent.at[put, c],
                recv.at[sem, c],
                dp=2 * ((x + k) % 4) + z,
            )

    def spread_rows(c, source, landing, put, sem):
        for k in (2, 1, 3):
            mm = (m + k) % 4
            send(
                source.at[c, pl.ds(pl.multiple_of(mm * OWN, OWN), OWN)],
                landing.at[c, k - 1],
                sent.at[put, c],
                recv.at[sem, c],
                mp=mm,
            )

    def hand_on(c, source, landing, put, sem, to):
        for k in (2, 1, 3, 0):
            send(
                source.at[c],
                landing.at[c, mine],
                sent.at[put, c],
                recv.at[sem, c],
                pipe=to,
                mp=(m + k) % 4,
            )

    def deliver(c, source, landing, put, sem):
        start = c * ROWS
        dd = start // 128
        row = pl.multiple_of(start % 128 + m * OWN, OWN)
        send_or_copy(
            (dd == d) & (x == m),
            source.at[c],
            landing.at[pl.ds(row, OWN), pl.ds(pl.multiple_of(z * BLK, LANES), BLK)],
            sent.at[put, c],
            once.at[sem],
            dp=dd,
            mp=x,
        )

    def total_pieces(c, own, others):
        return (own[c, 0].astype(F32) + others[c, 0].astype(F32)) + (
            others[c, 1].astype(F32) + others[c, 2].astype(F32)
        )

    def total_rows(c, own, others):
        return (own[c, mine].astype(F32) + others[c, 0].astype(F32)) + (
            others[c, 1].astype(F32) + others[c, 2].astype(F32)
        )

    def forward_1(c):
        await_bytes(hid.at[c], recv.at[H_IN, c])
        here = hid[c]
        wide = here.astype(F32)
        mean = jnp.sum(wide, axis=1, keepdims=True) * (1.0 / BLK)
        centered = wide - mean
        stats[c, 0] = to_rows(mean, jnp.sum(centered * centered, axis=1, keepdims=True))
        for k in range(1, 8):
            send(
                stats.at[c, 0],
                stats.at[c, k],
                sent.at[ST, c],
                recv.at[ST_IN, c],
                dp=(d + k) % 8,
            )
        for k in (2, 1, 3, 0):
            cols = cols_of((x + k) % 4)
            product = jnp.dot(here, wv[0, :, cols], preferred_element_type=F32)
            part[c, k] = (product - mean * sums[0:1, cols]).astype(BF16)
        spread_pieces(c, part, part_in, PO, P_IN)

    def forward_2(c):
        await_bytes(part_in.at[c], recv.at[P_IN, c])
        total = total_pieces(c, part, part_in)
        vals[c] = total
        swap[c] = total.astype(BF16)
        send(swap.at[c], swap_in.at[c], sent.at[SW, c], recv.at[S_IN, c], dp=2 * x + 1 - z)

    def forward_3(c):
        await_bytes(stats.at[c, pl.ds(1, 7)], recv.at[ST_IN, c])
        means = [stats[c, k, 0:1, :] for k in range(8)]
        squares = [stats[c, k, 1:2, :] for k in range(8)]
        mean = functools.reduce(lambda a, b: a + b, means) * 0.125
        square = functools.reduce(lambda a, b: a + b, squares)
        for k in range(8):
            gap = means[k] - mean
            square = square + float(BLK) * gap * gap
            tile[k : k + 1, :] = gap
        tile[8:9, :] = mean
        tile[9:10, :] = lax.rsqrt(square * (1.0 / WIDTH) + EPSILON)
        columns = tile[...].T[:ROWS]
        norm[c] = columns
        shift = columns[:, 0:1] * sums_in[0, 0:1, :]
        for k in range(1, 8):
            shift = shift + columns[:, k : k + 1] * sums_in[k, 0:1, :]
        await_bytes(swap_in.at[c], recv.at[S_IN, c])
        value = (vals[c] + swap_in[c].astype(F32) + shift) * columns[:, 9:10]
        vals[c] = value
        rounded = value.astype(BF16)
        for b in range(ROWS // MBT):
            for k in range(3):
                mixed[c, x, b * MBT : (b + 1) * MBT, k * LANES : (k + 1) * LANES] = jnp.dot(
                    table[0, k],
                    rounded[b * MBT : (b + 1) * MBT, k * LANES : (k + 1) * LANES],
                    preferred_element_type=F32,
                ).astype(BF16)
        gather_pieces(c, mixed, MX, M_IN)

    def forward_4(c):
        await_bytes(mixed.at[c, pl.ds(0, 3)], recv.at[M_IN, c])
        whole = jnp.concatenate([mixed[c, k] for k in range(4)], axis=1)
        branch[c] = jnp.dot(whole, wo[0], preferred_element_type=F32).astype(BF16)
        spread_rows(c, branch, branch_in, YO, Y_IN)

    def forward_5(c):
        await_bytes(branch_in.at[c], recv.at[Y_IN, c])
        total = total_rows(c, branch, branch_in)
        hid_out[c] = (hid[c, mine].astype(F32) + total).astype(BF16)

        @pl.when(p < SECTIONS - 1)
        def _():
            hand_on(c, hid_out, hid, HO, H_IN, p + 1)

        deliver(c, hid_out, out_land, OO, OUT_R)

    run_phases(
        FORWARD_ORDER,
        {1: forward_1, 2: forward_2, 3: forward_3, 4: forward_4, 5: forward_5},
    )

    sum_all = sums_in[0, 0:1, :]
    for k in range(1, 8):
        sum_all = sum_all + sums_in[k, 0:1, :]
    sums_in[0, 0:1, :] = sum_all

    def backward_1(c):
        await_bytes(grad.at[c], recv.at[G_IN, c])
        here = grad[c]
        for k in (2, 1, 3, 0):
            rows = cols_of((x + k) % 4)
            gpart[c, k] = lax.dot_general(
                here, wo[0, rows, :], (((1,), (1,)), ((), ())), preferred_element_type=F32
            ).astype(BF16)
        spread_pieces(c, gpart, gpart_in, GPO, GP_IN)

    def backward_2(c):
        await_bytes(gpart_in.at[c], recv.at[GP_IN, c])
        gswap[c] = total_pieces(c, gpart, gpart_in).astype(BF16)
        send(gswap.at[c], gswap_in.at[c], sent.at[GSW, c], recv.at[GS_IN, c], dp=2 * x + 1 - z)

    def backward_3(c):
        await_bytes(gswap_in.at[c], recv.at[GS_IN, c])
        total = gswap[c].astype(F32) + gswap_in[c].astype(F32)
        rounded = total.astype(BF16)
        for b in range(ROWS // MBT):
            for k in range(3):
                vgrad[c, x, b * MBT : (b + 1) * MBT, k * LANES : (k + 1) * LANES] = jnp.dot(
                    table[1, k],
                    rounded[b * MBT : (b + 1) * MBT, k * LANES : (k + 1) * LANES],
                    preferred_element_type=F32,
                ).astype(BF16)
        gather_pieces(c, vgrad, VX, V_IN)
        wide = vgrad[c, x].astype(F32)
        abx[c, 0] = to_rows(
            jnp.sum(wide * sums_in[0, 0:1, :], axis=1, keepdims=True),
            jnp.sum(wide * vals[c], axis=1, keepdims=True),
        )
        for k in (2, 1, 3):
            send(
                abx.at[c, 0],
                abx.at[c, k],
                sent.at[AX, c],
                recv.at[AX_IN, c],
                dp=2 * ((x + k) % 4) + z,
            )

    def backward_4(c):
        await_bytes(abx.at[c, pl.ds(1, 3)], recv.at[AX_IN, c])
        aby[c] = (abx[c, 0] + abx[c, 1]) + (abx[c, 2] + abx[c, 3])
        for k in (2, 1, 3):
            send(aby.at[c], aby_in.at[c, k - 1], sent.at[AY, c], recv.at[AY_IN, c], mp=(m + k) % 4)
        await_bytes(vgrad.at[c, pl.ds(0, 3)], recv.at[V_IN, c])
        whole = jnp.concatenate([vgrad[c, k] for k in range(4)], axis=1)
        gbranch[c] = lax.dot_general(
            whole, wv[0], (((1,), (1,)), ((), ())), preferred_element_type=F32
        ).astype(BF16)
        spread_rows(c, gbranch, gbranch_in, GYO, GY_IN)

    def backward_5(c):
        await_bytes(aby_in.at[c], recv.at[AY_IN, c])
        tile[0:8, :] = ((aby[c] + aby_in[c, 0]) + (aby_in[c, 1] + aby_in[c, 2])) * (1.0 / WIDTH)
        tile[...] = tile[...].T
        means = tile[mine, :]
        columns = norm[c, mine, :]
        inverse = columns[:, 9:10]
        scaled = (hid[c, mine].astype(F32) - columns[:, 8:9]) * inverse
        await_bytes(gbranch_in.at[c], recv.at[GY_IN, c])
        total = total_rows(c, gbranch, gbranch_in)
        change = inverse * (total - means[:, 0:1] - scaled * means[:, 1:2])
        grad_out[c] = (grad[c, mine].astype(F32) + change).astype(BF16)

        @pl.when(p > 0)
        def _():
            hand_on(c, grad_out, grad, GO, G_IN, p - 1)

        deliver(c, grad_out, grad_land, GOO, GOUT_R)

    def transposed(c):
        start = pl.multiple_of(c * LANES, LANES)
        group = LANES // ROWS
        left = []
        for k in range(group):
            columns = norm[c * group + k]
            wide = hid[c * group + k].astype(F32)
            left.append((wide - columns[:, 8:9]) * columns[:, 9:10])
        normed = jnp.concatenate(left, axis=0).astype(BF16)
        normed_t[:, pl.ds(start, LANES)] = normed.T
        for x_at in range(4):
            rows = jnp.concatenate([mixed[c * group + k, x_at] for k in range(group)], axis=0)
            mixed_t[x_at * PIECE : (x_at + 1) * PIECE, pl.ds(start, LANES)] = rows.T

    @pl.loop(0, TOKENS // LANES)
    def _(c):
        transposed(c)

    run_phases(
        BACKWARD_ORDER,
        {1: backward_1, 2: backward_2, 3: backward_3, 4: backward_4, 5: backward_5},
    )

    whole_grad = grad[...].reshape(TOKENS, BLK)

    @pl.loop(0, 6)
    def _(k):
        rows = pl.ds(pl.multiple_of(k * 256, 256), 256)
        output_grad[0, rows, :] = jnp.dot(
            mixed_t[rows, :], whole_grad, preferred_element_type=F32
        ).astype(BF16)

    for x_at in range(4):
        right = vgrad[:, x_at].reshape(TOKENS, PIECE)

        @pl.loop(0, 3)
        def _(k):
            rows = pl.ds(pl.multiple_of(k * 256, 256), 256)
            value_grad[0, rows, x_at * PIECE : (x_at + 1) * PIECE] = jnp.dot(
                normed_t[rows, :], right, preferred_element_type=F32
            ).astype(BF16)

    await_bytes(out_land, once.at[OUT_R])
    seg_out[...] = out_land[...]
    await_bytes(grad_land, once.at[GOUT_R])
    seg_grad[...] = grad_land[...]

    await_bytes(sums_in.at[pl.ds(1, 7)], once.at[SUMS_S])

    @pl.when((p == 0) | (p == SECTIONS - 1))
    def _():
        for _ in range(14):
            await_bytes(acts.at[0, :, pl.ds(0, BLK)], once.at[FIRST_S])

        @pl.when(x != m)
        def _():
            for _ in range(2):
                await_bytes(acts.at[0, :, pl.ds(0, BLK)], once.at[FIRST_S])

    def drain(c, carry):
        await_bytes(stats.at[c, pl.ds(1, 7)], sent.at[ST, c])
        await_bytes(part_in.at[c], sent.at[PO, c])
        await_bytes(swap.at[c], sent.at[SW, c])
        await_bytes(mixed.at[c, pl.ds(0, 3)], sent.at[MX, c])
        await_bytes(branch_in.at[c], sent.at[YO, c])
        await_bytes(gpart_in.at[c], sent.at[GPO, c])
        await_bytes(gswap.at[c], sent.at[GSW, c])
        await_bytes(vgrad.at[c, pl.ds(0, 3)], sent.at[VX, c])
        await_bytes(gbranch_in.at[c], sent.at[GYO, c])
        await_bytes(abx.at[c, pl.ds(1, 3)], sent.at[AX, c])
        await_bytes(aby_in.at[c], sent.at[AY, c])

        @pl.when(p < SECTIONS - 1)
        def _():
            await_bytes(hid.at[c], sent.at[HO, c])

        @pl.when(p > 0)
        def _():
            await_bytes(grad.at[c], sent.at[GO, c])

        @pl.when(jnp.logical_not((c * ROWS // 128 == d) & (x == m)))
        def _():
            await_bytes(hid_out.at[c], sent.at[OO, c])
            await_bytes(grad_out.at[c], sent.at[GOO, c])

        return carry

    lax.fori_loop(0, CHUNKS, drain, 0)


def shards(acts, out_grad, value_weight, output_weight, decay):
    vmem = pl.BlockSpec(memory_space=pltpu.VMEM)
    way = [
        pltpu.VMEM((CHUNKS, ROWS, BLK), BF16),
        pltpu.VMEM((CHUNKS, 4, ROWS, PIECE), BF16),
        pltpu.VMEM((CHUNKS, 3, ROWS, PIECE), BF16),
        pltpu.VMEM((CHUNKS, ROWS, PIECE), BF16),
        pltpu.VMEM((CHUNKS, ROWS, PIECE), BF16),
        pltpu.VMEM((CHUNKS, 4, ROWS, PIECE), BF16),
        pltpu.VMEM((CHUNKS, ROWS, BLK), BF16),
        pltpu.VMEM((CHUNKS, 3, OWN, BLK), BF16),
        pltpu.VMEM((CHUNKS, OWN, BLK), BF16),
        pltpu.VMEM((128, VAL), BF16),
    ]
    scratch = [
        *way,
        *way,
        pltpu.VMEM((CHUNKS, 8, 8, LANES), F32),
        pltpu.VMEM((8, VAL), F32),
        pltpu.VMEM((8, 8, PIECE), F32),
        pltpu.VMEM((CHUNKS, ROWS, PIECE), F32),
        pltpu.VMEM((CHUNKS, ROWS, LANES), F32),
        pltpu.VMEM((CHUNKS, 4, 8, LANES), F32),
        pltpu.VMEM((CHUNKS, 8, LANES), F32),
        pltpu.VMEM((CHUNKS, 3, 8, LANES), F32),
        pltpu.VMEM((2, 3, MBT, MBT), BF16),
        pltpu.VMEM((LANES, LANES), F32),
        pltpu.VMEM((BLK, TOKENS), BF16),
        pltpu.VMEM((VAL, TOKENS), BF16),
        pltpu.SemaphoreType.DMA((13, CHUNKS)),
        pltpu.SemaphoreType.DMA((15, CHUNKS)),
        pltpu.SemaphoreType.DMA((5,)),
    ]
    flops = 6 * 2 * TOKENS * BLK * VAL
    seg_out, seg_grad, value_grad, output_grad = pl.pallas_call(
        kernel,
        out_shape=(
            jax.ShapeDtypeStruct((128, VAL), BF16),
            jax.ShapeDtypeStruct((128, VAL), BF16),
            jax.ShapeDtypeStruct((1, BLK, VAL), BF16),
            jax.ShapeDtypeStruct((1, VAL, BLK), BF16),
        ),
        in_specs=[vmem, vmem, vmem, vmem, pl.BlockSpec(memory_space=pltpu.SMEM)],
        out_specs=(vmem, vmem, vmem, vmem),
        scratch_shapes=scratch,
        compiler_params=pltpu.CompilerParams(
            collective_id=0, has_side_effects=True, vmem_limit_bytes=62 * 1024 * 1024
        ),
        cost_estimate=pl.CostEstimate(flops=flops, bytes_accessed=12_000_000, transcendentals=0),
    )(acts, out_grad, value_weight, output_weight, decay)
    shape = (1, 2, MBT, VAL)
    return seg_out.reshape(shape), seg_grad.reshape(shape), value_grad, output_grad


def solution(mesh):
    in_specs = (
        P("dp", None, "mp"),
        P("dp", None, "mp"),
        P("pipe", "dp", "mp"),
        P("pipe", "mp", "dp"),
        P("pipe", "mp"),
    )
    out_specs = (
        P("pipe", "dp", None, "mp"),
        P("pipe", "dp", None, "mp"),
        P("pipe", "dp", "mp"),
        P("pipe", "mp", "dp"),
    )
    return jax.shard_map(shards, mesh=mesh, in_specs=in_specs, out_specs=out_specs, check_vma=False)
```

```python
import functools

import jax
import jax.numpy as jnp
from jax import lax
from jax.experimental import pallas as pl
from jax.experimental.pallas import tpu as pltpu
from jax.sharding import PartitionSpec as P

EPSILON = 1e-05
F32 = jnp.float32
BF16 = jnp.bfloat16
MESH = pl.DeviceIdType.MESH

TOKENS = 1024
MBT = 64
ROWS = 64
CHUNKS = TOKENS // ROWS
OWN = ROWS // 4
WIDTH = 6144
BLK = 768
VAL = 1536
PIECE = 384
SECTIONS = 8
LANES = 128

LAST_FORWARD = 20
BACKWARD_START = (12, 21, 21)


def send(src, dst, send_sem, recv_sem, **device):
    pltpu.make_async_remote_copy(
        src_ref=src,
        dst_ref=dst,
        send_sem=send_sem,
        recv_sem=recv_sem,
        device_id=device,
        device_id_type=MESH,
    ).start()


def await_bytes(ref, sem):
    pltpu.make_async_copy(ref, ref, sem).wait()


def send_or_copy(here, src, dst, send_sem, recv_sem, **device):
    @pl.when(here)
    def _():
        pltpu.make_async_copy(src, dst, recv_sem).start()

    @pl.when(jnp.logical_not(here))
    def _():
        send(src, dst, send_sem, recv_sem, **device)


def to_rows(first, second):
    lane = lax.broadcasted_iota(jnp.int32, (ROWS, LANES), 1)
    tile = jnp.where(lane == 0, first, jnp.where(lane == 1, second, 0.0))
    if ROWS < LANES:
        tile = jnp.concatenate([tile, jnp.zeros((LANES - ROWS, LANES), F32)], axis=0)
    return tile.T[:8]


def kernel(
    acts,
    out_grad,
    wv,
    wo,
    decay,
    seg_out,
    seg_grad,
    value_grad,
    output_grad,
    hid,
    part,
    part_in,
    swap,
    swap_in,
    mixed,
    branch,
    branch_in,
    hid_out,
    out_land,
    grad,
    gpart,
    gpart_in,
    gswap,
    gswap_in,
    vgrad,
    gbranch,
    gbranch_in,
    grad_out,
    grad_land,
    stats,
    sums,
    sums_in,
    sums_all,
    vals,
    norm,
    abx,
    aby,
    aby_in,
    table,
    tile,
    normed_t,
    mixed_t,
    recv,
    sent,
    once,
):
    p = lax.axis_index("pipe")
    d = lax.axis_index("dp")
    m = lax.axis_index("mp")
    x = d // 2
    z = d % 2
    (H_IN, ST_IN, P_IN, S_IN, M_IN, Y_IN, G_IN, GP_IN, GS_IN, V_IN, GY_IN, AX_IN, AY_IN) = range(13)
    (ST, PO, SW, MX, YO, HO, OO, GPO, GSW, VX, GYO, GO, GOO, AX, AY) = range(15)
    SUMS_R, OUT_R, GOUT_R, SUMS_S, FIRST_S = range(5)

    def cols_of(which):
        return pl.ds(pl.multiple_of(which * PIECE, LANES), PIECE)

    mine = pl.ds(pl.multiple_of(m * OWN, OWN), OWN)

    barrier = pltpu.get_barrier_semaphore()

    def greet(k, carry):
        dd = (d + k // 4) % 8
        mm = (m + k % 4) % 4
        pl.semaphore_signal(barrier, inc=1, device_id={"dp": dd, "mp": mm}, device_id_type=MESH)
        return carry

    lax.fori_loop(1, 32, greet, 0)

    @pl.when(p < SECTIONS - 1)
    def _():
        for k in range(4):
            pl.semaphore_signal(
                barrier, inc=1, device_id={"pipe": p + 1, "mp": (m + k) % 4}, device_id_type=MESH
            )

    @pl.when(p > 0)
    def _():
        for k in range(4):
            pl.semaphore_signal(
                barrier, inc=1, device_id={"pipe": p - 1, "mp": (m + k) % 4}, device_id_type=MESH
            )

    col_sum = jnp.sum(wv[0].astype(F32), axis=0, keepdims=True)
    sums[...] = jnp.broadcast_to(col_sum, (8, VAL))
    tile[...] = jnp.zeros((LANES, LANES), F32)
    row_id = lax.broadcasted_iota(jnp.int32, (MBT, MBT), 0).astype(F32)
    col_id = lax.broadcasted_iota(jnp.int32, (MBT, MBT), 1).astype(F32)
    for k in range(3):
        rate = jnp.full((MBT, MBT), decay[0, 3 * x + k], F32)
        scale = jnp.sqrt(1.0 - rate * rate)
        log_rate = jnp.log(rate)
        for way in range(2):
            offset = row_id - col_id if way == 0 else col_id - row_id
            power = jnp.exp(jnp.maximum(offset, 0.0) * log_rate) * scale
            table[way, k] = jnp.where(offset >= 0.0, power, 0.0).astype(BF16)

    inner = (p > 0) & (p < SECTIONS - 1)

    @pl.when(inner)
    def _():
        pl.semaphore_wait(barrier, 39)

    @pl.when(jnp.logical_not(inner))
    def _():
        pl.semaphore_wait(barrier, 35)

    def first_inputs(source, landing, sem):
        for b in range(2):
            start = (2 * d + b) * MBT
            chunk = start // ROWS
            row = pl.multiple_of(start % ROWS, MBT)
            for zz in range(2):
                for k in range(4):
                    dd = 2 * m + zz
                    mm = (m + k) % 4
                    send_or_copy(
                        (dd == d) & (mm == m),
                        source.at[b, :, pl.ds(zz * BLK, BLK)],
                        landing.at[chunk, pl.ds(row, MBT)],
                        once.at[FIRST_S],
                        recv.at[sem, chunk],
                        dp=dd,
                        mp=mm,
                    )

    @pl.when(p == 0)
    def _():
        first_inputs(acts, hid, H_IN)

    for k in range(1, 8):
        dd = (d + k) % 8
        send(
            sums.at[:, cols_of(dd // 2)],
            sums_in.at[k],
            once.at[SUMS_S],
            once.at[SUMS_R],
            dp=dd,
        )
    sums_in[0] = sums[:, cols_of(x)]

    @pl.when(p == SECTIONS - 1)
    def _():
        first_inputs(out_grad, grad, G_IN)

    await_bytes(sums_in.at[pl.ds(1, 7)], once.at[SUMS_R])
    sum_all = sums_in[0]
    for k in range(1, 8):
        sum_all = sum_all + sums_in[k]
    sums_all[...] = sum_all

    def spread_piece(c, k, source, landing, put, sem):
        send(
            source.at[c, k],
            landing.at[c, k - 1],
            sent.at[put, c],
            recv.at[sem, c],
            dp=2 * ((x + k) % 4) + z,
        )

    def gather_pieces(c, source, put, sem):
        for k in (2, 1, 3):
            send(
                source.at[c, x],
                source.at[c, x],
                sent.at[put, c],
                recv.at[sem, c],
                dp=2 * ((x + k) % 4) + z,
            )

    def spread_rows(c, source, landing, put, sem):
        for k in (2, 1, 3):
            mm = (m + k) % 4
            send(
                source.at[c, pl.ds(pl.multiple_of(mm * OWN, OWN), OWN)],
                landing.at[c, k - 1],
                sent.at[put, c],
                recv.at[sem, c],
                mp=mm,
            )

    def hand_on(c, source, landing, put, sem, to):
        for k in (2, 1, 3, 0):
            send(
                source.at[c],
                landing.at[c, mine],
                sent.at[put, c],
                recv.at[sem, c],
                pipe=to,
                mp=(m + k) % 4,
            )

    def deliver(c, source, landing, put, sem):
        start = c * ROWS
        dd = start // 128
        row = pl.multiple_of(start % 128 + m * OWN, OWN)
        send_or_copy(
            (dd == d) & (x == m),
            source.at[c],
            landing.at[pl.ds(row, OWN), pl.ds(pl.multiple_of(z * BLK, LANES), BLK)],
            sent.at[put, c],
            once.at[sem],
            dp=dd,
            mp=x,
        )

    def total_pieces(c, own, others):
        return (own[c, 0].astype(F32) + others[c, 0].astype(F32)) + (
            others[c, 1].astype(F32) + others[c, 2].astype(F32)
        )

    def total_rows(c, own, others):
        return (own[c, mine].astype(F32) + others[c, 0].astype(F32)) + (
            others[c, 1].astype(F32) + others[c, 2].astype(F32)
        )

    def means_1(c):
        wide = vgrad[c, x].astype(F32)
        abx[c, 0] = to_rows(
            jnp.sum(wide * sums_all[0:1, :], axis=1, keepdims=True),
            jnp.sum(wide * vals[c], axis=1, keepdims=True),
        )
        for k in (2, 1, 3):
            send(
                abx.at[c, 0],
                abx.at[c, k],
                sent.at[AX, c],
                recv.at[AX_IN, c],
                dp=2 * ((x + k) % 4) + z,
            )

    def means_2(c):
        await_bytes(abx.at[c, pl.ds(1, 3)], recv.at[AX_IN, c])
        aby[c] = (abx[c, 0] + abx[c, 1]) + (abx[c, 2] + abx[c, 3])
        for k in (2, 1, 3):
            send(aby.at[c], aby_in.at[c, k - 1], sent.at[AY, c], recv.at[AY_IN, c], mp=(m + k) % 4)

    def forward_1(c):
        await_bytes(hid.at[c], recv.at[H_IN, c])
        here = hid[c]
        wide = here.astype(F32)
        mean = jnp.sum(wide, axis=1, keepdims=True) * (1.0 / BLK)
        centered = wide - mean
        for k in (2, 1, 3, 0):
            cols = cols_of((x + k) % 4)
            product = jnp.dot(here, wv[0, :, cols], preferred_element_type=F32)
            part[c, k] = (product - mean * sums[0:1, cols]).astype(BF16)
            if k:
                spread_piece(c, k, part, part_in, PO, P_IN)
            if k == 1:
                stats[c, 0] = to_rows(mean, jnp.sum(centered * centered, axis=1, keepdims=True))
                for j in range(1, 8):
                    send(
                        stats.at[c, 0],
                        stats.at[c, j],
                        sent.at[ST, c],
                        recv.at[ST_IN, c],
                        dp=(d + j) % 8,
                    )

    def forward_2(c):
        await_bytes(part_in.at[c], recv.at[P_IN, c])
        total = total_pieces(c, part, part_in)
        vals[c] = total
        swap[c] = total.astype(BF16)
        send(swap.at[c], swap_in.at[c], sent.at[SW, c], recv.at[S_IN, c], dp=2 * x + 1 - z)

    def forward_3(c):
        await_bytes(stats.at[c, pl.ds(1, 7)], recv.at[ST_IN, c])
        means = [stats[c, k, 0:1, :] for k in range(8)]
        squares = [stats[c, k, 1:2, :] for k in range(8)]
        mean = functools.reduce(lambda a, b: a + b, means) * 0.125
        square = functools.reduce(lambda a, b: a + b, squares)
        for k in range(8):
            gap = means[k] - mean
            square = square + float(BLK) * gap * gap
            tile[k : k + 1, :] = gap
        tile[8:9, :] = mean
        tile[9:10, :] = lax.rsqrt(square * (1.0 / WIDTH) + EPSILON)
        columns = tile[...].T[:ROWS]
        norm[c] = columns
        shift = columns[:, 0:1] * sums_in[0, 0:1, :]
        for k in range(1, 8):
            shift = shift + columns[:, k : k + 1] * sums_in[k, 0:1, :]
        await_bytes(swap_in.at[c], recv.at[S_IN, c])
        value = (vals[c] + swap_in[c].astype(F32) + shift) * columns[:, 9:10]
        vals[c] = value
        rounded = value.astype(BF16)
        for b in range(ROWS // MBT):
            for k in range(3):
                mixed[c, x, b * MBT : (b + 1) * MBT, k * LANES : (k + 1) * LANES] = jnp.dot(
                    table[0, k],
                    rounded[b * MBT : (b + 1) * MBT, k * LANES : (k + 1) * LANES],
                    preferred_element_type=F32,
                ).astype(BF16)
        gather_pieces(c, mixed, MX, M_IN)
        pl.when(p == SECTIONS - 1)(functools.partial(means_1, c))

    def forward_4(c):
        await_bytes(mixed.at[c, pl.ds(0, 3)], recv.at[M_IN, c])
        whole = jnp.concatenate([mixed[c, k] for k in range(4)], axis=1)
        branch[c] = jnp.dot(whole, wo[0], preferred_element_type=F32).astype(BF16)
        spread_rows(c, branch, branch_in, YO, Y_IN)
        pl.when(p == SECTIONS - 1)(functools.partial(means_2, c))

    def forward_5(c):
        await_bytes(branch_in.at[c], recv.at[Y_IN, c])
        total = total_rows(c, branch, branch_in)
        hid_out[c] = (hid[c, mine].astype(F32) + total).astype(BF16)

        @pl.when(p < SECTIONS - 1)
        def _():
            hand_on(c, hid_out, hid, HO, H_IN, p + 1)

        deliver(c, hid_out, out_land, OO, OUT_R)

    def backward_1(c):
        await_bytes(grad.at[c], recv.at[G_IN, c])
        here = grad[c]
        for k in (2, 1, 3, 0):
            rows = cols_of((x + k) % 4)
            gpart[c, k] = lax.dot_general(
                here, wo[0, rows, :], (((1,), (1,)), ((), ())), preferred_element_type=F32
            ).astype(BF16)
            if k:
                spread_piece(c, k, gpart, gpart_in, GPO, GP_IN)

    def backward_2(c):
        await_bytes(gpart_in.at[c], recv.at[GP_IN, c])
        gswap[c] = total_pieces(c, gpart, gpart_in).astype(BF16)
        send(gswap.at[c], gswap_in.at[c], sent.at[GSW, c], recv.at[GS_IN, c], dp=2 * x + 1 - z)

    def backward_3(c):
        await_bytes(gswap_in.at[c], recv.at[GS_IN, c])
        total = gswap[c].astype(F32) + gswap_in[c].astype(F32)
        rounded = total.astype(BF16)
        for b in range(ROWS // MBT):
            for k in range(3):
                vgrad[c, x, b * MBT : (b + 1) * MBT, k * LANES : (k + 1) * LANES] = jnp.dot(
                    table[1, k],
                    rounded[b * MBT : (b + 1) * MBT, k * LANES : (k + 1) * LANES],
                    preferred_element_type=F32,
                ).astype(BF16)
        gather_pieces(c, vgrad, VX, V_IN)
        pl.when(p < SECTIONS - 1)(functools.partial(means_1, c))

    def backward_4(c):
        await_bytes(vgrad.at[c, pl.ds(0, 3)], recv.at[V_IN, c])
        whole = jnp.concatenate([vgrad[c, k] for k in range(4)], axis=1)
        gbranch[c] = lax.dot_general(
            whole, wv[0], (((1,), (1,)), ((), ())), preferred_element_type=F32
        ).astype(BF16)
        spread_rows(c, gbranch, gbranch_in, GYO, GY_IN)
        pl.when(p < SECTIONS - 1)(functools.partial(means_2, c))

    def backward_5(c):
        await_bytes(aby_in.at[c], recv.at[AY_IN, c])
        tile[0:8, :] = ((aby[c] + aby_in[c, 0]) + (aby_in[c, 1] + aby_in[c, 2])) * (1.0 / WIDTH)
        tile[...] = tile[...].T
        means = tile[mine, :]
        columns = norm[c, mine, :]
        inverse = columns[:, 9:10]
        scaled = (hid[c, mine].astype(F32) - columns[:, 8:9]) * inverse
        await_bytes(gbranch_in.at[c], recv.at[GY_IN, c])
        total = total_rows(c, gbranch, gbranch_in)
        change = inverse * (total - means[:, 0:1] - scaled * means[:, 1:2])
        grad_out[c] = (grad[c, mine].astype(F32) + change).astype(BF16)

        @pl.when(p > 0)
        def _():
            hand_on(c, grad_out, grad, GO, G_IN, p - 1)

        deliver(c, grad_out, grad_land, GOO, GOUT_R)

    def transposed(c):
        start = pl.multiple_of(c * LANES, LANES)
        group = LANES // ROWS
        left = []
        for k in range(group):
            columns = norm[c * group + k]
            wide = hid[c * group + k].astype(F32)
            left.append((wide - columns[:, 8:9]) * columns[:, 9:10])
        normed = jnp.concatenate(left, axis=0).astype(BF16)
        normed_t[:, pl.ds(start, LANES)] = normed.T
        for x_at in range(4):
            rows = jnp.concatenate([mixed[c * group + k, x_at] for k in range(group)], axis=0)
            mixed_t[x_at * PIECE : (x_at + 1) * PIECE, pl.ds(start, LANES)] = rows.T

    def transposed_2(c):
        pl.when(c % (LANES // ROWS) == LANES // ROWS - 1)(
            functools.partial(transposed, c // (LANES // ROWS))
        )

    is_last = p == SECTIONS - 1
    ahead = jnp.where(is_last, LAST_FORWARD, 0)
    near, middle, far = BACKWARD_START
    behind = jnp.where(p == SECTIONS - 2, near, jnp.where(p == SECTIONS - 3, middle, far))
    start = jnp.where(is_last, 0, behind)
    finish = jnp.where(is_last, LAST_FORWARD, behind) + 4
    phases = (
        (forward_1, ahead),
        (forward_2, ahead + 1),
        (forward_3, ahead + 2),
        (forward_4, ahead + 3),
        (forward_5, ahead + 4),
        (transposed_2, ahead + 4),
        (backward_1, start),
        (backward_2, start + 1),
        (backward_3, start + 2),
        (backward_4, start + 3),
        (backward_5, finish),
    )

    def window(step, carry):
        for phase, lag in phases:
            chunk = step - lag
            pl.when((chunk >= 0) & (chunk < CHUNKS))(functools.partial(phase, chunk))
        return carry

    lax.fori_loop(0, finish + CHUNKS, window, 0)

    whole_grad = grad[...].reshape(TOKENS, BLK)

    @pl.loop(0, 6)
    def _(k):
        rows = pl.ds(pl.multiple_of(k * 256, 256), 256)
        output_grad[0, rows, :] = jnp.dot(
            mixed_t[rows, :], whole_grad, preferred_element_type=F32
        ).astype(BF16)

    for x_at in range(4):
        right = vgrad[:, x_at].reshape(TOKENS, PIECE)

        @pl.loop(0, 3)
        def _(k):
            rows = pl.ds(pl.multiple_of(k * 256, 256), 256)
            value_grad[0, rows, x_at * PIECE : (x_at + 1) * PIECE] = jnp.dot(
                normed_t[rows, :], right, preferred_element_type=F32
            ).astype(BF16)

    await_bytes(out_land, once.at[OUT_R])
    seg_out[...] = out_land[...]
    await_bytes(grad_land, once.at[GOUT_R])
    seg_grad[...] = grad_land[...]

    await_bytes(sums_in.at[pl.ds(1, 7)], once.at[SUMS_S])

    @pl.when((p == 0) | (p == SECTIONS - 1))
    def _():
        for _ in range(14):
            await_bytes(acts.at[0, :, pl.ds(0, BLK)], once.at[FIRST_S])

        @pl.when(x != m)
        def _():
            for _ in range(2):
                await_bytes(acts.at[0, :, pl.ds(0, BLK)], once.at[FIRST_S])

    def drain(c, carry):
        await_bytes(stats.at[c, pl.ds(1, 7)], sent.at[ST, c])
        await_bytes(part_in.at[c], sent.at[PO, c])
        await_bytes(swap.at[c], sent.at[SW, c])
        await_bytes(mixed.at[c, pl.ds(0, 3)], sent.at[MX, c])
        await_bytes(branch_in.at[c], sent.at[YO, c])
        await_bytes(gpart_in.at[c], sent.at[GPO, c])
        await_bytes(gswap.at[c], sent.at[GSW, c])
        await_bytes(vgrad.at[c, pl.ds(0, 3)], sent.at[VX, c])
        await_bytes(gbranch_in.at[c], sent.at[GYO, c])
        await_bytes(abx.at[c, pl.ds(1, 3)], sent.at[AX, c])
        await_bytes(aby_in.at[c], sent.at[AY, c])

        @pl.when(p < SECTIONS - 1)
        def _():
            await_bytes(hid.at[c], sent.at[HO, c])

        @pl.when(p > 0)
        def _():
            await_bytes(grad.at[c], sent.at[GO, c])

        @pl.when(jnp.logical_not((c * ROWS // 128 == d) & (x == m)))
        def _():
            await_bytes(hid_out.at[c], sent.at[OO, c])
            await_bytes(grad_out.at[c], sent.at[GOO, c])

        return carry

    lax.fori_loop(0, CHUNKS, drain, 0)


def shards(acts, out_grad, value_weight, output_weight, decay):
    vmem = pl.BlockSpec(memory_space=pltpu.VMEM)
    way = [
        pltpu.VMEM((CHUNKS, ROWS, BLK), BF16),
        pltpu.VMEM((CHUNKS, 4, ROWS, PIECE), BF16),
        pltpu.VMEM((CHUNKS, 3, ROWS, PIECE), BF16),
        pltpu.VMEM((CHUNKS, ROWS, PIECE), BF16),
        pltpu.VMEM((CHUNKS, ROWS, PIECE), BF16),
        pltpu.VMEM((CHUNKS, 4, ROWS, PIECE), BF16),
        pltpu.VMEM((CHUNKS, ROWS, BLK), BF16),
        pltpu.VMEM((CHUNKS, 3, OWN, BLK), BF16),
        pltpu.VMEM((CHUNKS, OWN, BLK), BF16),
        pltpu.VMEM((128, VAL), BF16),
    ]
    scratch = [
        *way,
        *way,
        pltpu.VMEM((CHUNKS, 8, 8, LANES), F32),
        pltpu.VMEM((8, VAL), F32),
        pltpu.VMEM((8, 8, PIECE), F32),
        pltpu.VMEM((8, PIECE), F32),
        pltpu.VMEM((CHUNKS, ROWS, PIECE), F32),
        pltpu.VMEM((CHUNKS, ROWS, LANES), F32),
        pltpu.VMEM((CHUNKS, 4, 8, LANES), F32),
        pltpu.VMEM((CHUNKS, 8, LANES), F32),
        pltpu.VMEM((CHUNKS, 3, 8, LANES), F32),
        pltpu.VMEM((2, 3, MBT, MBT), BF16),
        pltpu.VMEM((LANES, LANES), F32),
        pltpu.VMEM((BLK, TOKENS), BF16),
        pltpu.VMEM((VAL, TOKENS), BF16),
        pltpu.SemaphoreType.DMA((13, CHUNKS)),
        pltpu.SemaphoreType.DMA((15, CHUNKS)),
        pltpu.SemaphoreType.DMA((5,)),
    ]
    flops = 6 * 2 * TOKENS * BLK * VAL
    seg_out, seg_grad, value_grad, output_grad = pl.pallas_call(
        kernel,
        out_shape=(
            jax.ShapeDtypeStruct((128, VAL), BF16),
            jax.ShapeDtypeStruct((128, VAL), BF16),
            jax.ShapeDtypeStruct((1, BLK, VAL), BF16),
            jax.ShapeDtypeStruct((1, VAL, BLK), BF16),
        ),
        in_specs=[vmem, vmem, vmem, vmem, pl.BlockSpec(memory_space=pltpu.SMEM)],
        out_specs=(vmem, vmem, vmem, vmem),
        scratch_shapes=scratch,
        compiler_params=pltpu.CompilerParams(
            collective_id=0, has_side_effects=True, vmem_limit_bytes=62 * 1024 * 1024
        ),
        cost_estimate=pl.CostEstimate(flops=flops, bytes_accessed=12_000_000, transcendentals=0),
    )(acts, out_grad, value_weight, output_weight, decay)
    shape = (1, 2, MBT, VAL)
    return seg_out.reshape(shape), seg_grad.reshape(shape), value_grad, output_grad


def solution(mesh):
    in_specs = (
        P("dp", None, "mp"),
        P("dp", None, "mp"),
        P("pipe", "dp", "mp"),
        P("pipe", "mp", "dp"),
        P("pipe", "mp"),
    )
    out_specs = (
        P("pipe", "dp", None, "mp"),
        P("pipe", "dp", None, "mp"),
        P("pipe", "dp", "mp"),
        P("pipe", "mp", "dp"),
    )
    return jax.shard_map(shards, mesh=mesh, in_specs=in_specs, out_specs=out_specs, check_vma=False)
```

```python
import functools

import jax
import jax.numpy as jnp
from jax import lax
from jax.experimental import pallas as pl
from jax.experimental.pallas import tpu as pltpu
from jax.sharding import PartitionSpec as P

EPSILON = 1e-05
F32 = jnp.float32
BF16 = jnp.bfloat16
MESH = pl.DeviceIdType.MESH

TOKENS = 1024
MBT = 64
ROWS = 64
CHUNKS = TOKENS // ROWS
OWN = ROWS // 4
WIDTH = 6144
BLK = 768
VAL = 1536
PIECE = 384
SECTIONS = 8
LANES = 128

LAST_FORWARD = 20
RELAY_AHEAD = 2
BACKWARD_START = (11, 20, 20)


def send(src, dst, send_sem, recv_sem, **device):
    pltpu.make_async_remote_copy(
        src_ref=src,
        dst_ref=dst,
        send_sem=send_sem,
        recv_sem=recv_sem,
        device_id=device,
        device_id_type=MESH,
    ).start()


def await_bytes(ref, sem):
    pltpu.make_async_copy(ref, ref, sem).wait()


def send_or_copy(here, src, dst, send_sem, recv_sem, **device):
    @pl.when(here)
    def _():
        pltpu.make_async_copy(src, dst, recv_sem).start()

    @pl.when(jnp.logical_not(here))
    def _():
        send(src, dst, send_sem, recv_sem, **device)


def to_rows(first, second):
    lane = lax.broadcasted_iota(jnp.int32, (ROWS, LANES), 1)
    tile = jnp.where(lane == 0, first, jnp.where(lane == 1, second, 0.0))
    if ROWS < LANES:
        tile = jnp.concatenate([tile, jnp.zeros((LANES - ROWS, LANES), F32)], axis=0)
    return tile.T[:8]


def kernel(
    acts,
    out_grad,
    wv,
    wo,
    decay,
    seg_out,
    seg_grad,
    value_grad,
    output_grad,
    hid,
    part,
    part_in,
    swap,
    swap_in,
    mixed,
    branch,
    branch_in,
    hid_out,
    out_land,
    grad,
    gpart,
    gpart_in,
    gswap,
    gswap_in,
    vgrad,
    gbranch,
    gbranch_in,
    grad_out,
    grad_land,
    stats,
    sums,
    sums_in,
    sums_all,
    vals,
    norm,
    abx,
    aby,
    aby_in,
    table,
    tile,
    normed_t,
    mixed_t,
    wv_t,
    wo_t,
    recv,
    sent,
    once,
):
    p = lax.axis_index("pipe")
    d = lax.axis_index("dp")
    m = lax.axis_index("mp")
    x = d // 2
    z = d % 2
    (H_IN, ST_IN, P_IN, S_IN, M_IN, Y_IN, G_IN, GP_IN, GS_IN, V_IN, GY_IN, AX_IN, AY_IN) = range(13)
    (ST, PO, SW, MX, YO, HO, OO, GPO, GSW, VX, GYO, GO, GOO, AX, AY, RL) = range(16)
    SUMS_R, OUT_R, GOUT_R, SUMS_S, FIRST_S = range(5)

    def cols_of(which):
        return pl.ds(pl.multiple_of(which * PIECE, LANES), PIECE)

    mine = pl.ds(pl.multiple_of(m * OWN, OWN), OWN)

    barrier = pltpu.get_barrier_semaphore()

    def greet(k, carry):
        dd = (d + k // 4) % 8
        mm = (m + k % 4) % 4
        pl.semaphore_signal(barrier, inc=1, device_id={"dp": dd, "mp": mm}, device_id_type=MESH)
        return carry

    lax.fori_loop(1, 32, greet, 0)

    @pl.when(p < SECTIONS - 1)
    def _():
        for k in range(4):
            pl.semaphore_signal(
                barrier, inc=1, device_id={"pipe": p + 1, "mp": (m + k) % 4}, device_id_type=MESH
            )

    @pl.when(p > 0)
    def _():
        for k in range(4):
            pl.semaphore_signal(
                barrier, inc=1, device_id={"pipe": p - 1, "mp": (m + k) % 4}, device_id_type=MESH
            )

    col_sum = jnp.sum(wv[0].astype(F32), axis=0, keepdims=True)
    sums[...] = jnp.broadcast_to(col_sum, (8, VAL))
    tile[...] = jnp.zeros((LANES, LANES), F32)
    row_id = lax.broadcasted_iota(jnp.int32, (MBT, MBT), 0).astype(F32)
    col_id = lax.broadcasted_iota(jnp.int32, (MBT, MBT), 1).astype(F32)
    for k in range(3):
        rate = jnp.full((MBT, MBT), decay[0, 3 * x + k], F32)
        scale = jnp.sqrt(1.0 - rate * rate)
        log_rate = jnp.log(rate)
        for way in range(2):
            offset = row_id - col_id if way == 0 else col_id - row_id
            power = jnp.exp(jnp.maximum(offset, 0.0) * log_rate) * scale
            table[way, k] = jnp.where(offset >= 0.0, power, 0.0).astype(BF16)

    inner = (p > 0) & (p < SECTIONS - 1)

    @pl.when(inner)
    def _():
        pl.semaphore_wait(barrier, 39)

    @pl.when(jnp.logical_not(inner))
    def _():
        pl.semaphore_wait(barrier, 35)

    def first_inputs(source, landing, sem, rows):
        for b in range(2):
            start = (2 * d + b) * MBT
            chunk = start // ROWS
            row = pl.multiple_of(start % ROWS, MBT)
            for zz in range(2):
                for k in range(rows):
                    dd = 2 * m + zz
                    mm = (m + k) % 4
                    send_or_copy(
                        (dd == d) & (mm == m),
                        source.at[b, :, pl.ds(zz * BLK, BLK)],
                        landing.at[chunk, pl.ds(row, MBT)],
                        once.at[FIRST_S],
                        recv.at[sem, chunk],
                        dp=dd,
                        mp=mm,
                    )

    for k in range(1, 8):
        dd = (d + k) % 8
        send(
            sums.at[:, cols_of(dd // 2)],
            sums_in.at[k],
            once.at[SUMS_S],
            once.at[SUMS_R],
            dp=dd,
        )
    sums_in[0] = sums[:, cols_of(x)]

    @pl.when(p == 0)
    def _():
        first_inputs(acts, hid, H_IN, 1)

    @pl.when(p == SECTIONS - 1)
    def _():
        first_inputs(out_grad, grad, G_IN, 4)

    def whole_sums():
        await_bytes(sums_in.at[pl.ds(1, 7)], once.at[SUMS_R])
        sum_all = sums_in[0]
        for k in range(1, 8):
            sum_all = sum_all + sums_in[k]
        sums_all[...] = sum_all

    def spread_piece(c, k, source, landing, put, sem):
        send(
            source.at[c, k],
            landing.at[c, k - 1],
            sent.at[put, c],
            recv.at[sem, c],
            dp=2 * ((x + k) % 4) + z,
        )

    def gather_pieces(c, source, put, sem):
        for k in (2, 1, 3):
            send(
                source.at[c, x],
                source.at[c, x],
                sent.at[put, c],
                recv.at[sem, c],
                dp=2 * ((x + k) % 4) + z,
            )

    def spread_rows(c, source, landing, put, sem):
        for k in (2, 1, 3):
            mm = (m + k) % 4
            send(
                source.at[c, pl.ds(pl.multiple_of(mm * OWN, OWN), OWN)],
                landing.at[c, k - 1],
                sent.at[put, c],
                recv.at[sem, c],
                mp=mm,
            )

    def hand_on(c, source, landing, put, sem, to):
        for k in (2, 1, 3, 0):
            send(
                source.at[c],
                landing.at[c, mine],
                sent.at[put, c],
                recv.at[sem, c],
                pipe=to,
                mp=(m + k) % 4,
            )

    def deliver(c, source, landing, put, sem):
        start = c * ROWS
        dd = start // 128
        row = pl.multiple_of(start % 128 + m * OWN, OWN)
        send_or_copy(
            (dd == d) & (x == m),
            source.at[c],
            landing.at[pl.ds(row, OWN), pl.ds(pl.multiple_of(z * BLK, LANES), BLK)],
            sent.at[put, c],
            once.at[sem],
            dp=dd,
            mp=x,
        )

    def total_pieces(c, own, others):
        return (own[c, 0].astype(F32) + others[c, 0].astype(F32)) + (
            others[c, 1].astype(F32) + others[c, 2].astype(F32)
        )

    def total_rows(c, own, others):
        return (own[c, mine].astype(F32) + others[c, 0].astype(F32)) + (
            others[c, 1].astype(F32) + others[c, 2].astype(F32)
        )

    def means_1(c):
        wide = vgrad[c, x].astype(F32)
        abx[c, 0] = to_rows(
            jnp.sum(wide * sums_all[0:1, :], axis=1, keepdims=True),
            jnp.sum(wide * vals[c], axis=1, keepdims=True),
        )
        for k in (2, 1, 3):
            send(
                abx.at[c, 0],
                abx.at[c, k],
                sent.at[AX, c],
                recv.at[AX_IN, c],
                dp=2 * ((x + k) % 4) + z,
            )

    def means_2(c):
        await_bytes(abx.at[c, pl.ds(1, 3)], recv.at[AX_IN, c])
        aby[c] = (abx[c, 0] + abx[c, 1]) + (abx[c, 2] + abx[c, 3])
        for k in (2, 1, 3):
            send(aby.at[c], aby_in.at[c, k - 1], sent.at[AY, c], recv.at[AY_IN, c], mp=(m + k) % 4)

    def flip():
        @pl.loop(0, VAL // LANES)
        def _(k):
            at = pl.ds(pl.multiple_of(k * LANES, LANES), LANES)
            wo_t[:, at] = wo[0, at, :].T
            wv_t[at, :] = wv[0, :, at].T

    pl.when(p > 0)(flip)

    relays = (p == 0) & (x == m)

    def relay(c):
        await_bytes(hid.at[c], recv.at[H_IN, c])
        for k in (2, 1, 3):
            send(
                hid.at[c],
                hid.at[c],
                sent.at[RL, c],
                recv.at[H_IN, c],
                mp=(m + k) % 4,
            )

    @pl.when(relays)
    def _():
        for c in range(RELAY_AHEAD):
            relay(c)

    def forward_1(c):
        pl.when(relays & (c < CHUNKS - RELAY_AHEAD))(functools.partial(relay, c + RELAY_AHEAD))

        @pl.when(jnp.logical_not(relays))
        def _():
            await_bytes(hid.at[c], recv.at[H_IN, c])

        here = hid[c]
        wide = here.astype(F32)
        mean = jnp.sum(wide, axis=1, keepdims=True) * (1.0 / BLK)
        centered = wide - mean
        for k in (2, 1, 3, 0):
            cols = cols_of((x + k) % 4)
            product = jnp.dot(here, wv[0, :, cols], preferred_element_type=F32)
            part[c, k] = (product - mean * sums[0:1, cols]).astype(BF16)
            if k:
                spread_piece(c, k, part, part_in, PO, P_IN)
            if k == 1:
                stats[c, 0] = to_rows(mean, jnp.sum(centered * centered, axis=1, keepdims=True))
                for j in range(1, 8):
                    send(
                        stats.at[c, 0],
                        stats.at[c, j],
                        sent.at[ST, c],
                        recv.at[ST_IN, c],
                        dp=(d + j) % 8,
                    )

    def forward_2(c):
        await_bytes(part_in.at[c], recv.at[P_IN, c])
        total = total_pieces(c, part, part_in)
        vals[c] = total
        swap[c] = total.astype(BF16)
        send(swap.at[c], swap_in.at[c], sent.at[SW, c], recv.at[S_IN, c], dp=2 * x + 1 - z)

    def forward_3(c):
        pl.when(c == 0)(whole_sums)
        await_bytes(stats.at[c, pl.ds(1, 7)], recv.at[ST_IN, c])
        means = [stats[c, k, 0:1, :] for k in range(8)]
        squares = [stats[c, k, 1:2, :] for k in range(8)]
        mean = functools.reduce(lambda a, b: a + b, means) * 0.125
        square = functools.reduce(lambda a, b: a + b, squares)
        for k in range(8):
            gap = means[k] - mean
            square = square + float(BLK) * gap * gap
            tile[k : k + 1, :] = gap
        tile[8:9, :] = mean
        tile[9:10, :] = lax.rsqrt(square * (1.0 / WIDTH) + EPSILON)
        columns = tile[...].T[:ROWS]
        norm[c] = columns
        shift = columns[:, 0:1] * sums_in[0, 0:1, :]
        for k in range(1, 8):
            shift = shift + columns[:, k : k + 1] * sums_in[k, 0:1, :]
        await_bytes(swap_in.at[c], recv.at[S_IN, c])
        value = (vals[c] + swap_in[c].astype(F32) + shift) * columns[:, 9:10]
        vals[c] = value
        rounded = value.astype(BF16)
        for b in range(ROWS // MBT):
            for k in range(3):
                mixed[c, x, b * MBT : (b + 1) * MBT, k * LANES : (k + 1) * LANES] = jnp.dot(
                    table[0, k],
                    rounded[b * MBT : (b + 1) * MBT, k * LANES : (k + 1) * LANES],
                    preferred_element_type=F32,
                ).astype(BF16)
        gather_pieces(c, mixed, MX, M_IN)
        pl.when(p == SECTIONS - 1)(functools.partial(means_1, c))

    def forward_4(c):
        await_bytes(mixed.at[c, pl.ds(0, 3)], recv.at[M_IN, c])
        whole = jnp.concatenate([mixed[c, k] for k in range(4)], axis=1)
        branch[c] = jnp.dot(whole, wo[0], preferred_element_type=F32).astype(BF16)
        spread_rows(c, branch, branch_in, YO, Y_IN)
        pl.when(p == SECTIONS - 1)(functools.partial(means_2, c))

    def forward_5(c):
        await_bytes(branch_in.at[c], recv.at[Y_IN, c])
        total = total_rows(c, branch, branch_in)
        hid_out[c] = (hid[c, mine].astype(F32) + total).astype(BF16)

        @pl.when(p < SECTIONS - 1)
        def _():
            hand_on(c, hid_out, hid, HO, H_IN, p + 1)

        deliver(c, hid_out, out_land, OO, OUT_R)

    def output_weights():
        @pl.loop(0, 6)
        def _(k):
            rows = pl.ds(pl.multiple_of(k * 256, 256), 256)
            output_grad[0, rows, :] = jnp.dot(
                mixed_t[rows, :], grad[...].reshape(TOKENS, BLK), preferred_element_type=F32
            ).astype(BF16)

    def value_weights():
        for x_at in range(4):

            @pl.loop(0, 3)
            def _(k):
                rows = pl.ds(pl.multiple_of(k * 256, 256), 256)
                value_grad[0, rows, x_at * PIECE : (x_at + 1) * PIECE] = jnp.dot(
                    normed_t[rows, :],
                    vgrad[:, x_at].reshape(TOKENS, PIECE),
                    preferred_element_type=F32,
                ).astype(BF16)

    def backward_1(c):
        await_bytes(grad.at[c], recv.at[G_IN, c])
        here = grad[c]
        for k in (2, 1, 3, 0):
            cols = cols_of((x + k) % 4)
            gpart[c, k] = jnp.dot(
                here, wo_t[:, cols], preferred_element_type=F32
            ).astype(BF16)
            if k:
                spread_piece(c, k, gpart, gpart_in, GPO, GP_IN)

    def backward_2(c):
        await_bytes(gpart_in.at[c], recv.at[GP_IN, c])
        gswap[c] = total_pieces(c, gpart, gpart_in).astype(BF16)
        send(gswap.at[c], gswap_in.at[c], sent.at[GSW, c], recv.at[GS_IN, c], dp=2 * x + 1 - z)
        pl.when((p == 0) & (c == CHUNKS - 1))(output_weights)

    def backward_3(c):
        await_bytes(gswap_in.at[c], recv.at[GS_IN, c])
        total = gswap[c].astype(F32) + gswap_in[c].astype(F32)
        rounded = total.astype(BF16)
        for b in range(ROWS // MBT):
            for k in range(3):
                vgrad[c, x, b * MBT : (b + 1) * MBT, k * LANES : (k + 1) * LANES] = jnp.dot(
                    table[1, k],
                    rounded[b * MBT : (b + 1) * MBT, k * LANES : (k + 1) * LANES],
                    preferred_element_type=F32,
                ).astype(BF16)
        gather_pieces(c, vgrad, VX, V_IN)
        pl.when(p < SECTIONS - 1)(functools.partial(means_1, c))

    def backward_4(c):
        await_bytes(vgrad.at[c, pl.ds(0, 3)], recv.at[V_IN, c])
        whole = jnp.concatenate([vgrad[c, k] for k in range(4)], axis=1)
        gbranch[c] = jnp.dot(whole, wv_t[...], preferred_element_type=F32).astype(BF16)
        spread_rows(c, gbranch, gbranch_in, GYO, GY_IN)
        pl.when(p < SECTIONS - 1)(functools.partial(means_2, c))
        pl.when((p == 0) & (c == CHUNKS - 1))(value_weights)

    def backward_5(c):
        await_bytes(aby_in.at[c], recv.at[AY_IN, c])
        tile[0:8, :] = ((aby[c] + aby_in[c, 0]) + (aby_in[c, 1] + aby_in[c, 2])) * (1.0 / WIDTH)
        tile[...] = tile[...].T
        means = tile[mine, :]
        columns = norm[c, mine, :]
        inverse = columns[:, 9:10]
        scaled = (hid[c, mine].astype(F32) - columns[:, 8:9]) * inverse
        await_bytes(gbranch_in.at[c], recv.at[GY_IN, c])
        total = total_rows(c, gbranch, gbranch_in)
        change = inverse * (total - means[:, 0:1] - scaled * means[:, 1:2])
        grad_out[c] = (grad[c, mine].astype(F32) + change).astype(BF16)

        @pl.when(p > 0)
        def _():
            hand_on(c, grad_out, grad, GO, G_IN, p - 1)

        deliver(c, grad_out, grad_land, GOO, GOUT_R)

    def transposed(c):
        start = pl.multiple_of(c * LANES, LANES)
        group = LANES // ROWS
        left = []
        for k in range(group):
            columns = norm[c * group + k]
            wide = hid[c * group + k].astype(F32)
            left.append((wide - columns[:, 8:9]) * columns[:, 9:10])
        normed = jnp.concatenate(left, axis=0).astype(BF16)
        normed_t[:, pl.ds(start, LANES)] = normed.T
        for x_at in range(4):
            rows = jnp.concatenate([mixed[c * group + k, x_at] for k in range(group)], axis=0)
            mixed_t[x_at * PIECE : (x_at + 1) * PIECE, pl.ds(start, LANES)] = rows.T

    def transposed_2(c):
        pl.when(c % (LANES // ROWS) == LANES // ROWS - 1)(
            functools.partial(transposed, c // (LANES // ROWS))
        )

    is_last = p == SECTIONS - 1
    ahead = jnp.where(is_last, LAST_FORWARD, 0)
    near, middle, far = BACKWARD_START
    behind = jnp.where(p == SECTIONS - 2, near, jnp.where(p == SECTIONS - 3, middle, far))
    start = jnp.where(is_last, 0, behind)
    finish = jnp.where(is_last, LAST_FORWARD, behind) + 4
    phases = (
        (forward_1, ahead),
        (forward_2, ahead + 1),
        (forward_3, ahead + 2),
        (forward_4, ahead + 3),
        (forward_5, ahead + 4),
        (transposed_2, ahead + 4),
        (backward_1, start),
        (backward_2, start + 1),
        (backward_3, start + 2),
        (backward_4, start + 3),
        (backward_5, finish),
    )

    def window(step, carry):
        pl.when((p == 0) & (step == CHUNKS + 4))(flip)
        for phase, lag in phases:
            chunk = step - lag
            pl.when((chunk >= 0) & (chunk < CHUNKS))(functools.partial(phase, chunk))
        return carry

    lax.fori_loop(0, finish + CHUNKS, window, 0)

    pl.when(p > 0)(output_weights)
    pl.when(p > 0)(value_weights)

    await_bytes(out_land, once.at[OUT_R])
    for b in range(2):
        seg_out[0, b] = out_land[b * MBT : (b + 1) * MBT]
    await_bytes(grad_land, once.at[GOUT_R])
    for b in range(2):
        seg_grad[0, b] = grad_land[b * MBT : (b + 1) * MBT]

    await_bytes(sums_in.at[pl.ds(1, 7)], once.at[SUMS_S])

    def first_sent(count):
        for _ in range(count):
            await_bytes(acts.at[0, :, pl.ds(0, BLK)], once.at[FIRST_S])

    pl.when(p == 0)(functools.partial(first_sent, 2))
    pl.when(p == SECTIONS - 1)(functools.partial(first_sent, 14))
    pl.when(((p == 0) | (p == SECTIONS - 1)) & (x != m))(functools.partial(first_sent, 2))

    def drain(c, carry):
        await_bytes(stats.at[c, pl.ds(1, 7)], sent.at[ST, c])
        await_bytes(part_in.at[c], sent.at[PO, c])
        await_bytes(swap.at[c], sent.at[SW, c])
        await_bytes(mixed.at[c, pl.ds(0, 3)], sent.at[MX, c])
        await_bytes(branch_in.at[c], sent.at[YO, c])
        await_bytes(gpart_in.at[c], sent.at[GPO, c])
        await_bytes(gswap.at[c], sent.at[GSW, c])
        await_bytes(vgrad.at[c, pl.ds(0, 3)], sent.at[VX, c])
        await_bytes(gbranch_in.at[c], sent.at[GYO, c])
        await_bytes(abx.at[c, pl.ds(1, 3)], sent.at[AX, c])
        await_bytes(aby_in.at[c], sent.at[AY, c])

        @pl.when(relays)
        def _():
            for _ in range(3):
                await_bytes(hid.at[c], sent.at[RL, c])

        @pl.when(p < SECTIONS - 1)
        def _():
            await_bytes(hid.at[c], sent.at[HO, c])

        @pl.when(p > 0)
        def _():
            await_bytes(grad.at[c], sent.at[GO, c])

        @pl.when(jnp.logical_not((c * ROWS // 128 == d) & (x == m)))
        def _():
            await_bytes(hid_out.at[c], sent.at[OO, c])
            await_bytes(grad_out.at[c], sent.at[GOO, c])

        return carry

    lax.fori_loop(0, CHUNKS, drain, 0)


def shards(acts, out_grad, value_weight, output_weight, decay):
    vmem = pl.BlockSpec(memory_space=pltpu.VMEM)
    way = [
        pltpu.VMEM((CHUNKS, ROWS, BLK), BF16),
        pltpu.VMEM((CHUNKS, 4, ROWS, PIECE), BF16),
        pltpu.VMEM((CHUNKS, 3, ROWS, PIECE), BF16),
        pltpu.VMEM((CHUNKS, ROWS, PIECE), BF16),
        pltpu.VMEM((CHUNKS, ROWS, PIECE), BF16),
        pltpu.VMEM((CHUNKS, 4, ROWS, PIECE), BF16),
        pltpu.VMEM((CHUNKS, ROWS, BLK), BF16),
        pltpu.VMEM((CHUNKS, 3, OWN, BLK), BF16),
        pltpu.VMEM((CHUNKS, OWN, BLK), BF16),
        pltpu.VMEM((128, VAL), BF16),
    ]
    scratch = [
        *way,
        *way,
        pltpu.VMEM((CHUNKS, 8, 8, LANES), F32),
        pltpu.VMEM((8, VAL), F32),
        pltpu.VMEM((8, 8, PIECE), F32),
        pltpu.VMEM((8, PIECE), F32),
        pltpu.VMEM((CHUNKS, ROWS, PIECE), F32),
        pltpu.VMEM((CHUNKS, ROWS, LANES), F32),
        pltpu.VMEM((CHUNKS, 4, 8, LANES), F32),
        pltpu.VMEM((CHUNKS, 8, LANES), F32),
        pltpu.VMEM((CHUNKS, 3, 8, LANES), F32),
        pltpu.VMEM((2, 3, MBT, MBT), BF16),
        pltpu.VMEM((LANES, LANES), F32),
        pltpu.VMEM((BLK, TOKENS), BF16),
        pltpu.VMEM((VAL, TOKENS), BF16),
        pltpu.VMEM((VAL, BLK), BF16),
        pltpu.VMEM((BLK, VAL), BF16),
        pltpu.SemaphoreType.DMA((13, CHUNKS)),
        pltpu.SemaphoreType.DMA((16, CHUNKS)),
        pltpu.SemaphoreType.DMA((5,)),
    ]
    flops = 6 * 2 * TOKENS * BLK * VAL
    return pl.pallas_call(
        kernel,
        out_shape=(
            jax.ShapeDtypeStruct((1, 2, MBT, VAL), BF16),
            jax.ShapeDtypeStruct((1, 2, MBT, VAL), BF16),
            jax.ShapeDtypeStruct((1, BLK, VAL), BF16),
            jax.ShapeDtypeStruct((1, VAL, BLK), BF16),
        ),
        in_specs=[vmem, vmem, vmem, vmem, pl.BlockSpec(memory_space=pltpu.SMEM)],
        out_specs=(vmem, vmem, vmem, vmem),
        scratch_shapes=scratch,
        compiler_params=pltpu.CompilerParams(
            collective_id=0, has_side_effects=True, vmem_limit_bytes=62 * 1024 * 1024
        ),
        cost_estimate=pl.CostEstimate(flops=flops, bytes_accessed=12_000_000, transcendentals=0),
    )(acts, out_grad, value_weight, output_weight, decay)


def solution(mesh):
    in_specs = (
        P("dp", None, "mp"),
        P("dp", None, "mp"),
        P("pipe", "dp", "mp"),
        P("pipe", "mp", "dp"),
        P("pipe", "mp"),
    )
    out_specs = (
        P("pipe", "dp", None, "mp"),
        P("pipe", "dp", None, "mp"),
        P("pipe", "dp", "mp"),
        P("pipe", "mp", "dp"),
    )
    return jax.shard_map(shards, mesh=mesh, in_specs=in_specs, out_specs=out_specs, check_vma=False)
```

```python
import functools

import jax
import jax.numpy as jnp
from jax import lax
from jax.experimental import pallas as pl
from jax.experimental.pallas import tpu as pltpu
from jax.sharding import PartitionSpec as P

EPSILON = 1e-05
F32 = jnp.float32
BF16 = jnp.bfloat16
MESH = pl.DeviceIdType.MESH

TOKENS = 1024
MBT = 64
ROWS = 64
CHUNKS = TOKENS // ROWS
OWN = ROWS // 4
WIDTH = 6144
BLK = 768
VAL = 1536
PIECE = 384
SECTIONS = 8
LANES = 128

LAST_FORWARD = 20
RELAY_AHEAD = 2
BACKWARD_START = (11, 20, 20)


def send(src, dst, send_sem, recv_sem, **device):
    pltpu.make_async_remote_copy(
        src_ref=src,
        dst_ref=dst,
        send_sem=send_sem,
        recv_sem=recv_sem,
        device_id=device,
        device_id_type=MESH,
    ).start()


def await_bytes(ref, sem):
    pltpu.make_async_copy(ref, ref, sem).wait()


def send_or_copy(here, src, dst, send_sem, recv_sem, **device):
    @pl.when(here)
    def _():
        pltpu.make_async_copy(src, dst, recv_sem).start()

    @pl.when(jnp.logical_not(here))
    def _():
        send(src, dst, send_sem, recv_sem, **device)


def to_rows(first, second):
    lane = lax.broadcasted_iota(jnp.int32, (ROWS, LANES), 1)
    tile = jnp.where(lane == 0, first, jnp.where(lane == 1, second, 0.0))
    if ROWS < LANES:
        tile = jnp.concatenate([tile, jnp.zeros((LANES - ROWS, LANES), F32)], axis=0)
    return tile.T[:8]


def kernel(
    acts,
    out_grad,
    wv,
    wo,
    decay,
    seg_out,
    seg_grad,
    value_grad,
    output_grad,
    hid,
    part,
    part_in,
    swap,
    swap_in,
    mixed,
    branch,
    branch_in,
    hid_out,
    out_land,
    grad,
    gpart,
    gpart_in,
    gswap,
    gswap_in,
    vgrad,
    gbranch,
    gbranch_in,
    grad_out,
    grad_land,
    stats,
    sums,
    sums_in,
    sums_all,
    vals,
    norm,
    abx,
    aby,
    aby_in,
    table,
    tile,
    normed_t,
    mixed_t,
    wv_t,
    wo_t,
    recv,
    sent,
    once,
):
    p = lax.axis_index("pipe")
    d = lax.axis_index("dp")
    m = lax.axis_index("mp")
    x = d // 2
    z = d % 2
    (H_IN, ST_IN, P_IN, S_IN, M_IN, Y_IN, G_IN, GP_IN, GS_IN, V_IN, GY_IN, AX_IN, AY_IN) = range(13)
    (ST, PO, SW, MX, YO, HO, OO, GPO, GSW, VX, GYO, GO, GOO, AX, AY, RL) = range(16)
    SUMS_R, OUT_R, GOUT_R, SUMS_S, FIRST_S = range(5)

    def cols_of(which):
        return pl.ds(pl.multiple_of(which * PIECE, LANES), PIECE)

    mine = pl.ds(pl.multiple_of(m * OWN, OWN), OWN)

    barrier = pltpu.get_barrier_semaphore()

    def greet(k, carry):
        dd = (d + k // 4) % 8
        mm = (m + k % 4) % 4
        pl.semaphore_signal(barrier, inc=1, device_id={"dp": dd, "mp": mm}, device_id_type=MESH)
        return carry

    lax.fori_loop(1, 32, greet, 0)

    @pl.when(p < SECTIONS - 1)
    def _():
        for k in range(4):
            pl.semaphore_signal(
                barrier, inc=1, device_id={"pipe": p + 1, "mp": (m + k) % 4}, device_id_type=MESH
            )

    @pl.when(p > 0)
    def _():
        for k in range(4):
            pl.semaphore_signal(
                barrier, inc=1, device_id={"pipe": p - 1, "mp": (m + k) % 4}, device_id_type=MESH
            )

    col_sum = jnp.sum(wv[0].astype(F32), axis=0, keepdims=True)
    sums[...] = jnp.broadcast_to(col_sum, (8, VAL))
    tile[...] = jnp.zeros((LANES, LANES), F32)
    row_id = lax.broadcasted_iota(jnp.int32, (MBT, MBT), 0).astype(F32)
    col_id = lax.broadcasted_iota(jnp.int32, (MBT, MBT), 1).astype(F32)
    for k in range(3):
        rate = jnp.full((MBT, MBT), decay[0, 3 * x + k], F32)
        scale = jnp.sqrt(1.0 - rate * rate)
        log_rate = jnp.log(rate)
        for way in range(2):
            offset = row_id - col_id if way == 0 else col_id - row_id
            power = jnp.exp(jnp.maximum(offset, 0.0) * log_rate) * scale
            table[way, k] = jnp.where(offset >= 0.0, power, 0.0).astype(BF16)

    inner = (p > 0) & (p < SECTIONS - 1)

    @pl.when(inner)
    def _():
        pl.semaphore_wait(barrier, 39)

    @pl.when(jnp.logical_not(inner))
    def _():
        pl.semaphore_wait(barrier, 35)

    def first_inputs(source, landing, sem, rows):
        for b in range(2):
            start = (2 * d + b) * MBT
            chunk = start // ROWS
            row = pl.multiple_of(start % ROWS, MBT)
            for zz in range(2):
                for k in range(rows):
                    dd = 2 * m + zz
                    mm = (m + k) % 4
                    send_or_copy(
                        (dd == d) & (mm == m),
                        source.at[b, :, pl.ds(zz * BLK, BLK)],
                        landing.at[chunk, pl.ds(row, MBT)],
                        once.at[FIRST_S],
                        recv.at[sem, chunk],
                        dp=dd,
                        mp=mm,
                    )

    for k in range(1, 8):
        dd = (d + k) % 8
        send(
            sums.at[:, cols_of(dd // 2)],
            sums_in.at[k],
            once.at[SUMS_S],
            once.at[SUMS_R],
            dp=dd,
        )
    sums_in[0] = sums[:, cols_of(x)]

    @pl.when(p == 0)
    def _():
        first_inputs(acts, hid, H_IN, 1)

    @pl.when(p == SECTIONS - 1)
    def _():
        first_inputs(out_grad, grad, G_IN, 4)

    def whole_sums():
        await_bytes(sums_in.at[pl.ds(1, 7)], once.at[SUMS_R])
        sum_all = sums_in[0]
        for k in range(1, 8):
            sum_all = sum_all + sums_in[k]
        sums_all[...] = sum_all

    def spread_piece(c, k, source, landing, put, sem):
        send(
            source.at[c, k],
            landing.at[c, k - 1],
            sent.at[put, c],
            recv.at[sem, c],
            dp=2 * ((x + k) % 4) + z,
        )

    def gather_pieces(c, source, put, sem):
        for k in (2, 1, 3):
            send(
                source.at[c, x],
                source.at[c, x],
                sent.at[put, c],
                recv.at[sem, c],
                dp=2 * ((x + k) % 4) + z,
            )

    def spread_rows(c, source, landing, put, sem):
        for k in (2, 1, 3):
            mm = (m + k) % 4
            send(
                source.at[c, pl.ds(pl.multiple_of(mm * OWN, OWN), OWN)],
                landing.at[c, k - 1],
                sent.at[put, c],
                recv.at[sem, c],
                mp=mm,
            )

    def hand_on(c, source, landing, put, sem, to):
        for k in (2, 1, 3, 0):
            send(
                source.at[c],
                landing.at[c, mine],
                sent.at[put, c],
                recv.at[sem, c],
                pipe=to,
                mp=(m + k) % 4,
            )

    def deliver(c, source, landing, put, sem):
        start = c * ROWS
        dd = start // 128
        row = pl.multiple_of(start % 128 + m * OWN, OWN)
        send_or_copy(
            (dd == d) & (x == m),
            source.at[c],
            landing.at[pl.ds(row, OWN), pl.ds(pl.multiple_of(z * BLK, LANES), BLK)],
            sent.at[put, c],
            once.at[sem],
            dp=dd,
            mp=x,
        )

    def total_pieces(c, own, others):
        return (own[c, 0].astype(F32) + others[c, 0].astype(F32)) + (
            others[c, 1].astype(F32) + others[c, 2].astype(F32)
        )

    def total_rows(c, own, others):
        return (own[c, mine].astype(F32) + others[c, 0].astype(F32)) + (
            others[c, 1].astype(F32) + others[c, 2].astype(F32)
        )

    def means_1(c):
        wide = vgrad[c, x].astype(F32)
        abx[c, 0] = to_rows(
            jnp.sum(wide * sums_all[0:1, :], axis=1, keepdims=True),
            jnp.sum(wide * vals[c], axis=1, keepdims=True),
        )
        for k in (2, 1, 3):
            send(
                abx.at[c, 0],
                abx.at[c, k],
                sent.at[AX, c],
                recv.at[AX_IN, c],
                dp=2 * ((x + k) % 4) + z,
            )

    def means_2(c):
        await_bytes(abx.at[c, pl.ds(1, 3)], recv.at[AX_IN, c])
        aby[c] = (abx[c, 0] + abx[c, 1]) + (abx[c, 2] + abx[c, 3])
        for k in (2, 1, 3):
            send(aby.at[c], aby_in.at[c, k - 1], sent.at[AY, c], recv.at[AY_IN, c], mp=(m + k) % 4)

    def flip():
        @pl.loop(0, VAL // LANES)
        def _(k):
            at = pl.ds(pl.multiple_of(k * LANES, LANES), LANES)
            wo_t[:, at] = wo[0, at, :].T
            wv_t[at, :] = wv[0, :, at].T

    pl.when(p > 0)(flip)

    relays = (p == 0) & (x == m)

    def relay(c):
        await_bytes(hid.at[c], recv.at[H_IN, c])
        for k in (2, 1, 3):
            send(
                hid.at[c],
                hid.at[c],
                sent.at[RL, c],
                recv.at[H_IN, c],
                mp=(m + k) % 4,
            )

    @pl.when(relays)
    def _():
        for c in range(RELAY_AHEAD):
            relay(c)

    def forward_1(c):
        pl.when(relays & (c < CHUNKS - RELAY_AHEAD))(functools.partial(relay, c + RELAY_AHEAD))

        @pl.when(jnp.logical_not(relays))
        def _():
            await_bytes(hid.at[c], recv.at[H_IN, c])

        here = hid[c]
        wide = here.astype(F32)
        mean = jnp.sum(wide, axis=1, keepdims=True) * (1.0 / BLK)
        centered = wide - mean
        for k in (2, 1, 3, 0):
            cols = cols_of((x + k) % 4)
            product = jnp.dot(here, wv[0, :, cols], preferred_element_type=F32)
            part[c, k] = (product - mean * sums[0:1, cols]).astype(BF16)
            if k:
                spread_piece(c, k, part, part_in, PO, P_IN)
            if k == 1:
                stats[c, 0] = to_rows(mean, jnp.sum(centered * centered, axis=1, keepdims=True))
                for j in range(1, 8):
                    send(
                        stats.at[c, 0],
                        stats.at[c, j],
                        sent.at[ST, c],
                        recv.at[ST_IN, c],
                        dp=(d + j) % 8,
                    )

    def forward_2(c):
        await_bytes(part_in.at[c], recv.at[P_IN, c])
        total = total_pieces(c, part, part_in)
        vals[c] = total
        swap[c] = total.astype(BF16)
        send(swap.at[c], swap_in.at[c], sent.at[SW, c], recv.at[S_IN, c], dp=2 * x + 1 - z)

    def forward_3(c):
        pl.when(c == 0)(whole_sums)
        await_bytes(stats.at[c, pl.ds(1, 7)], recv.at[ST_IN, c])
        means = [stats[c, k, 0:1, :] for k in range(8)]
        squares = [stats[c, k, 1:2, :] for k in range(8)]
        mean = functools.reduce(lambda a, b: a + b, means) * 0.125
        square = functools.reduce(lambda a, b: a + b, squares)
        for k in range(8):
            gap = means[k] - mean
            square = square + float(BLK) * gap * gap
            tile[k : k + 1, :] = gap
        tile[8:9, :] = mean
        tile[9:10, :] = lax.rsqrt(square * (1.0 / WIDTH) + EPSILON)
        columns = tile[...].T[:ROWS]
        norm[c] = columns
        shift = columns[:, 0:1] * sums_in[0, 0:1, :]
        for k in range(1, 8):
            shift = shift + columns[:, k : k + 1] * sums_in[k, 0:1, :]
        await_bytes(swap_in.at[c], recv.at[S_IN, c])
        value = (vals[c] + swap_in[c].astype(F32) + shift) * columns[:, 9:10]
        vals[c] = value
        rounded = value.astype(BF16)
        for b in range(ROWS // MBT):
            for k in range(3):
                mixed[c, x, b * MBT : (b + 1) * MBT, k * LANES : (k + 1) * LANES] = jnp.dot(
                    table[0, k],
                    rounded[b * MBT : (b + 1) * MBT, k * LANES : (k + 1) * LANES],
                    preferred_element_type=F32,
                ).astype(BF16)
        gather_pieces(c, mixed, MX, M_IN)
        pl.when(p == SECTIONS - 1)(functools.partial(means_1, c))

    def forward_4(c):
        await_bytes(mixed.at[c, pl.ds(0, 3)], recv.at[M_IN, c])
        whole = jnp.concatenate([mixed[c, k] for k in range(4)], axis=1)
        branch[c] = jnp.dot(whole, wo[0], preferred_element_type=F32).astype(BF16)
        spread_rows(c, branch, branch_in, YO, Y_IN)
        pl.when(p == SECTIONS - 1)(functools.partial(means_2, c))

    def forward_5(c):
        await_bytes(branch_in.at[c], recv.at[Y_IN, c])
        total = total_rows(c, branch, branch_in)
        hid_out[c] = (hid[c, mine].astype(F32) + total).astype(BF16)

        @pl.when(p < SECTIONS - 1)
        def _():
            hand_on(c, hid_out, hid, HO, H_IN, p + 1)

        deliver(c, hid_out, out_land, OO, OUT_R)

    def output_weights():
        @pl.loop(0, 6)
        def _(k):
            rows = pl.ds(pl.multiple_of(k * 256, 256), 256)
            output_grad[0, rows, :] = jnp.dot(
                mixed_t[rows, :], grad[...].reshape(TOKENS, BLK), preferred_element_type=F32
            ).astype(BF16)

    def value_weights():
        for x_at in range(4):

            @pl.loop(0, 3)
            def _(k):
                rows = pl.ds(pl.multiple_of(k * 256, 256), 256)
                value_grad[0, rows, x_at * PIECE : (x_at + 1) * PIECE] = jnp.dot(
                    normed_t[rows, :],
                    vgrad[:, x_at].reshape(TOKENS, PIECE),
                    preferred_element_type=F32,
                ).astype(BF16)

    def backward_1(c):
        await_bytes(grad.at[c], recv.at[G_IN, c])
        here = grad[c]
        for k in (2, 1, 3, 0):
            cols = cols_of((x + k) % 4)
            gpart[c, k] = jnp.dot(
                here, wo_t[:, cols], preferred_element_type=F32
            ).astype(BF16)
            if k:
                spread_piece(c, k, gpart, gpart_in, GPO, GP_IN)

    def backward_2(c):
        await_bytes(gpart_in.at[c], recv.at[GP_IN, c])
        gswap[c] = total_pieces(c, gpart, gpart_in).astype(BF16)
        send(gswap.at[c], gswap_in.at[c], sent.at[GSW, c], recv.at[GS_IN, c], dp=2 * x + 1 - z)
        pl.when((p == 0) & (c == CHUNKS - 1))(output_weights)

    def backward_3(c):
        await_bytes(gswap_in.at[c], recv.at[GS_IN, c])
        total = gswap[c].astype(F32) + gswap_in[c].astype(F32)
        rounded = total.astype(BF16)
        for b in range(ROWS // MBT):
            for k in range(3):
                vgrad[c, x, b * MBT : (b + 1) * MBT, k * LANES : (k + 1) * LANES] = jnp.dot(
                    table[1, k],
                    rounded[b * MBT : (b + 1) * MBT, k * LANES : (k + 1) * LANES],
                    preferred_element_type=F32,
                ).astype(BF16)
        gather_pieces(c, vgrad, VX, V_IN)
        pl.when(p < SECTIONS - 1)(functools.partial(means_1, c))

    def backward_4(c):
        await_bytes(vgrad.at[c, pl.ds(0, 3)], recv.at[V_IN, c])
        whole = jnp.concatenate([vgrad[c, k] for k in range(4)], axis=1)
        gbranch[c] = jnp.dot(whole, wv_t[...], preferred_element_type=F32).astype(BF16)
        spread_rows(c, gbranch, gbranch_in, GYO, GY_IN)
        pl.when(p < SECTIONS - 1)(functools.partial(means_2, c))
        pl.when((p == 0) & (c == CHUNKS - 1))(value_weights)

    def backward_5(c):
        await_bytes(aby_in.at[c], recv.at[AY_IN, c])
        tile[0:8, :] = ((aby[c] + aby_in[c, 0]) + (aby_in[c, 1] + aby_in[c, 2])) * (1.0 / WIDTH)
        tile[...] = tile[...].T
        means = tile[mine, :]
        columns = norm[c, mine, :]
        inverse = columns[:, 9:10]
        scaled = (hid[c, mine].astype(F32) - columns[:, 8:9]) * inverse
        await_bytes(gbranch_in.at[c], recv.at[GY_IN, c])
        total = total_rows(c, gbranch, gbranch_in)
        change = inverse * (total - means[:, 0:1] - scaled * means[:, 1:2])
        grad_out[c] = (grad[c, mine].astype(F32) + change).astype(BF16)

        @pl.when(p > 0)
        def _():
            hand_on(c, grad_out, grad, GO, G_IN, p - 1)

        deliver(c, grad_out, grad_land, GOO, GOUT_R)

    def transposed(c):
        start = pl.multiple_of(c * LANES, LANES)
        group = LANES // ROWS
        left = []
        for k in range(group):
            columns = norm[c * group + k]
            wide = hid[c * group + k].astype(F32)
            left.append((wide - columns[:, 8:9]) * columns[:, 9:10])
        normed = jnp.concatenate(left, axis=0).astype(BF16)
        normed_t[:, pl.ds(start, LANES)] = normed.T
        for x_at in range(4):
            rows = jnp.concatenate([mixed[c * group + k, x_at] for k in range(group)], axis=0)
            mixed_t[x_at * PIECE : (x_at + 1) * PIECE, pl.ds(start, LANES)] = rows.T

    def transposed_2(c):
        pl.when(c % (LANES // ROWS) == LANES // ROWS - 1)(
            functools.partial(transposed, c // (LANES // ROWS))
        )

    is_last = p == SECTIONS - 1
    ahead = jnp.where(is_last, LAST_FORWARD, 0)
    near, middle, far = BACKWARD_START
    behind = jnp.where(p == SECTIONS - 2, near, jnp.where(p == SECTIONS - 3, middle, far))
    start = jnp.where(is_last, 0, behind)
    finish = jnp.where(is_last, LAST_FORWARD, behind) + 4
    phases = (
        (backward_1, start),
        (backward_2, start + 1),
        (backward_3, start + 2),
        (backward_4, start + 3),
        (backward_5, finish),
        (forward_1, ahead),
        (forward_2, ahead + 1),
        (forward_3, ahead + 2),
        (forward_4, ahead + 3),
        (forward_5, ahead + 4),
        (transposed_2, ahead + 4),
    )

    def window(step, carry):
        pl.when((p == 0) & (step == CHUNKS + 4))(flip)
        for phase, lag in phases:
            chunk = step - lag
            pl.when((chunk >= 0) & (chunk < CHUNKS))(functools.partial(phase, chunk))
        return carry

    lax.fori_loop(0, finish + CHUNKS, window, 0)

    pl.when(p > 0)(output_weights)
    pl.when(p > 0)(value_weights)

    await_bytes(out_land, once.at[OUT_R])
    for b in range(2):
        seg_out[0, b] = out_land[b * MBT : (b + 1) * MBT]
    await_bytes(grad_land, once.at[GOUT_R])
    for b in range(2):
        seg_grad[0, b] = grad_land[b * MBT : (b + 1) * MBT]

    await_bytes(sums_in.at[pl.ds(1, 7)], once.at[SUMS_S])

    def first_sent(count):
        for _ in range(count):
            await_bytes(acts.at[0, :, pl.ds(0, BLK)], once.at[FIRST_S])

    pl.when(p == 0)(functools.partial(first_sent, 2))
    pl.when(p == SECTIONS - 1)(functools.partial(first_sent, 14))
    pl.when(((p == 0) | (p == SECTIONS - 1)) & (x != m))(functools.partial(first_sent, 2))

    def drain(c, carry):
        await_bytes(stats.at[c, pl.ds(1, 7)], sent.at[ST, c])
        await_bytes(part_in.at[c], sent.at[PO, c])
        await_bytes(swap.at[c], sent.at[SW, c])
        await_bytes(mixed.at[c, pl.ds(0, 3)], sent.at[MX, c])
        await_bytes(branch_in.at[c], sent.at[YO, c])
        await_bytes(gpart_in.at[c], sent.at[GPO, c])
        await_bytes(gswap.at[c], sent.at[GSW, c])
        await_bytes(vgrad.at[c, pl.ds(0, 3)], sent.at[VX, c])
        await_bytes(gbranch_in.at[c], sent.at[GYO, c])
        await_bytes(abx.at[c, pl.ds(1, 3)], sent.at[AX, c])
        await_bytes(aby_in.at[c], sent.at[AY, c])

        @pl.when(relays)
        def _():
            for _ in range(3):
                await_bytes(hid.at[c], sent.at[RL, c])

        @pl.when(p < SECTIONS - 1)
        def _():
            await_bytes(hid.at[c], sent.at[HO, c])

        @pl.when(p > 0)
        def _():
            await_bytes(grad.at[c], sent.at[GO, c])

        @pl.when(jnp.logical_not((c * ROWS // 128 == d) & (x == m)))
        def _():
            await_bytes(hid_out.at[c], sent.at[OO, c])
            await_bytes(grad_out.at[c], sent.at[GOO, c])

        return carry

    lax.fori_loop(0, CHUNKS, drain, 0)


def shards(acts, out_grad, value_weight, output_weight, decay):
    vmem = pl.BlockSpec(memory_space=pltpu.VMEM)
    way = [
        pltpu.VMEM((CHUNKS, ROWS, BLK), BF16),
        pltpu.VMEM((CHUNKS, 4, ROWS, PIECE), BF16),
        pltpu.VMEM((CHUNKS, 3, ROWS, PIECE), BF16),
        pltpu.VMEM((CHUNKS, ROWS, PIECE), BF16),
        pltpu.VMEM((CHUNKS, ROWS, PIECE), BF16),
        pltpu.VMEM((CHUNKS, 4, ROWS, PIECE), BF16),
        pltpu.VMEM((CHUNKS, ROWS, BLK), BF16),
        pltpu.VMEM((CHUNKS, 3, OWN, BLK), BF16),
        pltpu.VMEM((CHUNKS, OWN, BLK), BF16),
        pltpu.VMEM((128, VAL), BF16),
    ]
    scratch = [
        *way,
        *way,
        pltpu.VMEM((CHUNKS, 8, 8, LANES), F32),
        pltpu.VMEM((8, VAL), F32),
        pltpu.VMEM((8, 8, PIECE), F32),
        pltpu.VMEM((8, PIECE), F32),
        pltpu.VMEM((CHUNKS, ROWS, PIECE), F32),
        pltpu.VMEM((CHUNKS, ROWS, LANES), F32),
        pltpu.VMEM((CHUNKS, 4, 8, LANES), F32),
        pltpu.VMEM((CHUNKS, 8, LANES), F32),
        pltpu.VMEM((CHUNKS, 3, 8, LANES), F32),
        pltpu.VMEM((2, 3, MBT, MBT), BF16),
        pltpu.VMEM((LANES, LANES), F32),
        pltpu.VMEM((BLK, TOKENS), BF16),
        pltpu.VMEM((VAL, TOKENS), BF16),
        pltpu.VMEM((VAL, BLK), BF16),
        pltpu.VMEM((BLK, VAL), BF16),
        pltpu.SemaphoreType.DMA((13, CHUNKS)),
        pltpu.SemaphoreType.DMA((16, CHUNKS)),
        pltpu.SemaphoreType.DMA((5,)),
    ]
    flops = 6 * 2 * TOKENS * BLK * VAL
    return pl.pallas_call(
        kernel,
        out_shape=(
            jax.ShapeDtypeStruct((1, 2, MBT, VAL), BF16),
            jax.ShapeDtypeStruct((1, 2, MBT, VAL), BF16),
            jax.ShapeDtypeStruct((1, BLK, VAL), BF16),
            jax.ShapeDtypeStruct((1, VAL, BLK), BF16),
        ),
        in_specs=[vmem, vmem, vmem, vmem, pl.BlockSpec(memory_space=pltpu.SMEM)],
        out_specs=(vmem, vmem, vmem, vmem),
        scratch_shapes=scratch,
        compiler_params=pltpu.CompilerParams(
            collective_id=0, has_side_effects=True, vmem_limit_bytes=62 * 1024 * 1024
        ),
        cost_estimate=pl.CostEstimate(flops=flops, bytes_accessed=12_000_000, transcendentals=0),
    )(acts, out_grad, value_weight, output_weight, decay)


def solution(mesh):
    in_specs = (
        P("dp", None, "mp"),
        P("dp", None, "mp"),
        P("pipe", "dp", "mp"),
        P("pipe", "mp", "dp"),
        P("pipe", "mp"),
    )
    out_specs = (
        P("pipe", "dp", None, "mp"),
        P("pipe", "dp", None, "mp"),
        P("pipe", "dp", "mp"),
        P("pipe", "mp", "dp"),
    )
    return jax.shard_map(shards, mesh=mesh, in_specs=in_specs, out_specs=out_specs, check_vma=False)
```
